256 devices in a mesh: sec: 2 (over z_lo), gx: 8 (over x, core), row: 16 (over y, z_hi).
Axes of the slice: x: 4, y: 4, z: 8 (z_hi: 4, z_lo: 2; z = z_hi * 2 + z_lo), core: 2. Of those that a mesh axis runs over, the one named last changes fastest.
Arguments:
- les_density: float32 [128, 512, 256], P('gx', 'row', 'sec'), may hold values from 0.5 to 1.5
- les_rest: float32 [4, 128, 512, 256], P(None, 'gx', 'row', 'sec'), may hold values from -4 to 4
- acoustic: float32 [4, 64, 256, 256], P(None, 'gx', 'row', 'sec'), may hold values from -6 to 6
- block_owner: int32 [131072, 1], P(('sec', 'gx', 'row')), may hold values from 0 to 127; in each aligned block of 512 rows (0 to 511, 512 to 1023, ...) at most 10 rows name the same one
- block_weights: bfloat16 [131072, 64, 128], P(('sec', 'gx', 'row')), may hold values from -0.5 to 0.5
- block_counts: int32 [131072], P(('sec', 'gx', 'row')), may hold values from 32 to 128
- block_patch: int32 [131072], P(('sec', 'gx', 'row')), may hold values from 0 to 255
- tile_class: int32 [2, 8, 16], P('sec', 'gx', 'row'), may hold values from 0 to 3
- sample_index: int32 [32768], P(('sec', 'gx', 'row')), may hold values from 0 to 16383
- far_kernel: float32 [128, 32768], P(None, ('sec', 'gx', 'row')), may hold values from -0.03125 to 0.03125
Outputs:
- les_next: float32 [5, 128, 512, 256], P(None, 'gx', 'row', 'sec')
- acoustic_next: float32 [4, 64, 256, 256], P(None, 'gx', 'row', 'sec')
- far_field: float32 [128], replicated
The draws below stay inside these ranges and needn't reach their ends.
Inputs may be any that keep to these rules, and one draw needn't show every extreme that they name: `block_owner`: the rows of one device name no owner more than 10 times; some device's rows name some owner exactly 10 times.
All inputs are finite; a program needn't handle non-finite values.
Results may differ from the reference program's by a relative error of at most 0.0015.
Values sent between devices are 32-bit elements; how exact they have to be, the bound alone decides.
No kernel may reach another device: no remote copies, remote signals or barrier semaphores. Data moves between devices by JAX's collectives and lax.ppermute only.
A program may use at most 64 MiB of HBM per device.

```python
import math
import jax
import jax.numpy as jnp
import numpy as np
from jax import lax

LX = 16
LY = 32
LZ = 128
BLOCK_CELLS = 128
PATCH_CELLS = 64
SAMPLES_DEV = 128
OBSERVERS = 128
AX = 8
AY = 16
AZ = 128
NB = 512
NPATCH = 256
OWNERS = 128
CAP = 10
SECTIONS = 2
TILES_X = 8
TILES_R = 16
NX = 128
NY = 512
NZ = 256
WX = 64
WY = 256
WZ = 256
BLOCKS = 131072
SAMPLES = 32768
N_SEC = 2
N_GX = 8
N_ROW = 16
DEVICES = 256


def plant(array, stream_key, smallest, largest):
    dims = array.shape
    spot = [jax.random.randint(jax.random.fold_in(stream_key, axis), (), 0, dims[axis]) for axis in range(len(dims))]
    array = array.at[tuple(spot)].set(smallest)
    longest = dims.index(max(dims))
    spot[longest] = (spot[longest] + 1) % dims[longest]
    return array.at[tuple(spot)].set(largest)


def block_levels(key, extent, pieces, smallest, top_value):
    def one(dim, blocks):
        steps = jax.random.uniform(jax.random.fold_in(jax.random.fold_in(key, 6), dim), (blocks,), jnp.float32, smallest / len(pieces), top_value / len(pieces))
        return jnp.repeat(jnp.exp(steps), extent[dim] // blocks).reshape((-1,) + (1,) * (len(extent) - dim - 1))

    loudness = one(*pieces[0])
    for cut in pieces[1:]:
        loudness = loudness * one(*cut)
    return loudness


def deal_out(own_key, own, number, rows, count, top, bound, skew):
    sequence = jax.random.permutation(own_key, count)
    heavy_load, ordinary = portions_of(count, rows * top, bound, skew, True), portions_of(count, rows * top, bound, skew, False)
    places = jnp.arange(count)

    def named(tallies, turn):
        used = int((tallies > 0).sum())
        fixed = max(1, used // 4)
        moved = fixed + (places - fixed + turn * (used - fixed)) % max(1, count - fixed)
        return jnp.zeros((count,), jnp.int32).at[sequence[jnp.where(places < fixed, places, moved)]].set(jnp.asarray(tallies, jnp.int32))

    tallies = jnp.where(number % 4 == 0, named(heavy_load, number // 4), named(ordinary, number - number // 4 - 1))
    mixed = jax.random.permutation(jax.random.fold_in(own, 3), count)
    source_of, receiver = mixed[0:count // 2 * 2:2], mixed[1:count // 2 * 2:2]
    margin = jnp.minimum(tallies[source_of] - 1, bound - tallies[receiver]) // 2
    margin = jnp.where((source_of == sequence[0]) | (receiver == sequence[0]) | (tallies[receiver] == 0), 0, jnp.maximum(margin, 0))
    moved = jax.random.randint(jax.random.fold_in(own, 4), (count // 2,), 0, 1 << 20) % (margin + 1)
    tallies = tallies.at[source_of].add(-moved).at[receiver].add(moved)
    members = jnp.searchsorted(jnp.cumsum(tallies), jnp.arange(rows * top), side="right").astype(jnp.int32)
    grid = members.reshape(top, rows).T
    grid = grid[jax.random.permutation(jax.random.fold_in(own, 1), rows)]
    turn = jax.random.randint(jax.random.fold_in(own, 2), (rows, 1), 0, top)
    return jnp.take_along_axis(grid, (jnp.arange(top)[None, :] + turn) % top, axis=1)


def portions_of(amount, total, reach, slope, full):
    loads = [(1 << 20) // math.isqrt(rank ** slope) + 1 for rank in range(1, amount + 1)]
    largest = reach if full else min(reach, max(-(-total // amount), total * loads[0] // sum(loads)))
    least = 1 if total - largest >= amount - 1 else 0
    holding, rest = [largest] + [least] * (amount - 1), total - largest - least * (amount - 1)
    while rest > 0:
        movable = [i for i in range(1, amount) if holding[i] < largest] or [i for i in range(1, amount) if holding[i] < reach]
        mass, budget = sum([loads[i] for i in movable]), rest
        for i in movable:
            more = min(reach - holding[i], max(1, budget * loads[i] // mass), rest)
            holding[i] = holding[i] + more
            rest = rest - more
    return np.array(holding)


def scatter_about(stream_key, dims, scale, reach, shards=(), kind=jnp.bfloat16):
    array = jax.random.normal(stream_key, dims, jnp.float32) * scale
    if len(shards) > 0:
        array = block_levels(stream_key, dims, shards, -0.22, 0.18) * array
    return jnp.clip(array, min=-reach, max=reach).astype(kind)


def setup_inputs(seed: int = 0) -> dict:
    arg_keys = jax.random.split(jax.random.key(seed), 11)
    les_density = jnp.clip(0.5 + 1.0 * jax.random.uniform(arg_keys[0], (NX, NY, NZ), jnp.float32) ** block_levels(arg_keys[0], (NX, NY, NZ), ((0, 8), (1, 16), (2, 2)), -0.2, 0.2), 0.5, 1.5)
    les_rest = scatter_about(arg_keys[1], (4, NX, NY, NZ), 1.0, 4.0, ((1, 8), (2, 16), (3, 2)), jnp.float32)
    acoustic = scatter_about(arg_keys[2], (4, WX, WY, WZ), 1.0, 6.0, ((1, 8), (2, 16), (3, 2)), jnp.float32)
    block_owner_keys = jax.random.split(jax.random.fold_in(arg_keys[3], 1), BLOCKS // NB)
    block_owner_turns = jax.random.permutation(jax.random.fold_in(arg_keys[3], 3), BLOCKS // NB)
    block_owner = jax.vmap(lambda own, number: deal_out(jax.random.fold_in(arg_keys[3], 2), own, number, NB, OWNERS, 1, CAP, 2))(block_owner_keys, block_owner_turns).reshape((BLOCKS, 1))
    block_weights = scatter_about(arg_keys[4], (BLOCKS, PATCH_CELLS, BLOCK_CELLS), BLOCK_CELLS ** -0.5, 0.5, ((0, 256),))
    block_counts = plant(jax.random.randint(arg_keys[5], (BLOCKS,), BLOCK_CELLS // 4, BLOCK_CELLS + 1), jax.random.fold_in(arg_keys[5], 1), BLOCK_CELLS // 4, BLOCK_CELLS).astype(jnp.int32)
    block_patch = plant(jax.random.randint(arg_keys[6], (BLOCKS,), 0, NPATCH), jax.random.fold_in(arg_keys[6], 1), 0, NPATCH - 1).astype(jnp.int32)
    tile_class = plant(jax.random.randint(arg_keys[7], (SECTIONS, TILES_X, TILES_R), 0, 4), jax.random.fold_in(arg_keys[7], 1), 0, 3).astype(jnp.int32)
    sample_index = plant(jax.random.randint(arg_keys[8], (SAMPLES,), 0, AX * AY * AZ), jax.random.fold_in(arg_keys[8], 1), 0, (AX * AY * AZ) - 1).astype(jnp.int32)
    far_kernel = scatter_about(arg_keys[9], (OBSERVERS, SAMPLES), SAMPLES ** -0.5, 0.03125, ((1, 256),), jnp.float32)
    return {"les_density": les_density, "les_rest": les_rest, "acoustic": acoustic, "block_owner": block_owner, "block_weights": block_weights, "block_counts": block_counts, "block_patch": block_patch, "tile_class": tile_class, "sample_index": sample_index, "far_kernel": far_kernel}


LES_STEP = 0.2
WAVE_STEP = 0.25


def shifted(padded, direction, offset):
    selector = [slice(None), slice(1, -1), slice(1, -1), slice(1, -1)]
    selector[direction] = slice(offset, offset + padded.shape[direction] - 2)
    return padded[tuple(selector)]


def derive(padded, direction):
    return 0.5 * (shifted(padded, direction, 2) - shifted(padded, direction, 0))


def pad_cells(cell_field):
    return jnp.pad(cell_field, ((0, 0), (1, 1), (1, 1), (1, 1)))


def les_update(padded):
    les_state = padded[:5]
    flux_sum = derive(les_state * padded[5:6], 1)
    flux_sum = flux_sum + derive(les_state * padded[6:7], 2)
    flux_sum = flux_sum + derive(les_state * padded[7:8], 3)
    return shifted(les_state, 1, 1) - LES_STEP * flux_sum


def lamb_vector(velocity_pad):
    gradients = [[derive(velocity_pad[component:component + 1], spatial)[0] for spatial in (1, 2, 3)] for component in range(3)]
    speed = shifted(velocity_pad, 1, 1)
    swirl_x = gradients[2][1] - gradients[1][2]
    swirl_y = gradients[0][2] - gradients[2][0]
    swirl_z = gradients[1][0] - gradients[0][1]
    lamb_x = swirl_y * speed[2] - swirl_z * speed[1]
    lamb_y = swirl_z * speed[0] - swirl_x * speed[2]
    lamb_z = swirl_x * speed[1] - swirl_y * speed[0]
    return jnp.stack([lamb_x, lamb_y, lamb_z])


def wave_update(padded, mean_flow, stiffness, source):
    current = shifted(padded, 1, 1)
    along = [derive(padded[part:part + 1], 1)[0] for part in range(4)]
    pressure_grad = [along[0], derive(padded[0:1], 2)[0], derive(padded[0:1], 3)[0]]
    divergence = along[1] + derive(padded[2:3], 2)[0] + derive(padded[3:4], 3)[0]
    pressure = current[0] - WAVE_STEP * (mean_flow * along[0] + stiffness * divergence)
    layers = [pressure]
    for spatial in range(3):
        layers.append(current[1 + spatial] - WAVE_STEP * (mean_flow * along[1 + spatial] + pressure_grad[spatial] + source[spatial]))
    return jnp.stack(layers)


def cell_map(tile_values):
    spread = jnp.broadcast_to(tile_values.transpose(1, 2, 0)[:, None, :, None, :, None], (N_GX, AX, N_ROW, AY, N_SEC, AZ))
    return spread.reshape(WX, WY, WZ)


def reference(les_density, les_rest, acoustic, block_owner, block_weights, block_counts, block_patch, tile_class, sample_index, far_kernel):
    velocity = les_rest[0:3] / les_density[None]
    stacked = jnp.concatenate([les_density[None], les_rest, velocity], axis=0)
    padded = pad_cells(stacked)
    les_next = les_update(padded)
    lamb = lamb_vector(padded[5:8]).astype(jnp.bfloat16)
    lamb_tiles = lamb.reshape(3, N_GX, LX, N_ROW, LY, N_SEC, LZ).transpose(5, 1, 3, 0, 2, 4, 6).reshape(DEVICES, 3, NB, BLOCK_CELLS)
    weights = block_weights.reshape(DEVICES, NB, PATCH_CELLS, BLOCK_CELLS)
    counts = block_counts.reshape(DEVICES, NB)

    def interpolate(operands):
        lamb_tile, weight_tile, count_tile = operands
        valid_mask = jnp.arange(BLOCK_CELLS, dtype=jnp.int32)[None, None, :] < count_tile[:, None, None]
        masked = jnp.where(valid_mask, weight_tile, jnp.zeros_like(weight_tile))
        return jnp.einsum("ckb,kpb->kcp", lamb_tile.astype(jnp.float32), masked.astype(jnp.float32))

    payload = lax.map(interpolate, (lamb_tiles, weights, counts)).reshape(BLOCKS, 3 * PATCH_CELLS)
    block_device = jnp.arange(BLOCKS, dtype=jnp.int32) // NB
    target = (block_device // OWNERS) * OWNERS + block_owner[:, 0].astype(jnp.int32)
    segment = target * NPATCH + block_patch.astype(jnp.int32)
    source = jax.ops.segment_sum(payload, segment, num_segments=DEVICES * NPATCH)
    source = source.reshape(N_SEC, N_GX, N_ROW, NPATCH, 3, PATCH_CELLS).transpose(4, 0, 1, 2, 3, 5)
    source = source.reshape(3, N_SEC, N_GX, N_ROW, AX, AY, AZ).transpose(0, 2, 4, 3, 5, 1, 6).reshape(3, WX, WY, WZ)
    class_value = tile_class.astype(jnp.float32)
    mean_flow = cell_map(0.1 + 0.3 * class_value)
    stiffness = cell_map(1.0 + 0.25 * class_value)
    acoustic_next = wave_update(pad_cells(acoustic), mean_flow, stiffness, source)
    pressure_tiles = acoustic_next[0].reshape(N_GX, AX, N_ROW, AY, N_SEC, AZ).transpose(4, 0, 2, 1, 3, 5).reshape(DEVICES, AX * AY * AZ)
    samples = jnp.take_along_axis(pressure_tiles, sample_index.reshape(DEVICES, SAMPLES_DEV).astype(jnp.int32), axis=1).reshape(SAMPLES)
    far_field = jnp.dot(far_kernel, samples, precision=lax.Precision.HIGHEST)
    return les_next, acoustic_next, far_field
```

```python
import jax
import jax.numpy as jnp
from jax import lax
from jax.experimental import pallas as pl
from jax.experimental.pallas import tpu as pltpu
from jax.sharding import PartitionSpec as P

LES_STEP = 0.2
WAVE_STEP = 0.25
CAP = 10
ROWS = 16
F32 = jnp.float32
BF16 = jnp.bfloat16
ALL = ("sec", "gx", "row")
MIB = 1 << 20


def iota(shape, dim):
    return lax.broadcasted_iota(jnp.int32, shape, dim)


def as_column(line):
    return jnp.transpose(jnp.broadcast_to(line, (128, 128)))


def edge_line(block, high, eye):
    column = jnp.where(high, block[:, 127:128], block[:, 0:1])
    return jnp.sum(jnp.where(eye, column, 0.0), axis=0, keepdims=True)


def safe(density):
    return jnp.where(density == 0.0, 1.0, density)


def down(plane, halo):
    return jnp.where(iota(plane.shape, 0) == 0, halo, pltpu.roll(plane, 1, 0))


def up(plane, halo):
    last = plane.shape[0] - 1
    return jnp.where(iota(plane.shape, 0) == last, halo, pltpu.roll(plane, last, 0))


def derive_z(plane, halo, sec):
    lane = iota(plane.shape, 1)
    before = jnp.where(lane == 0, jnp.where(sec == 1, halo, 0.0), pltpu.roll(plane, 1, 1))
    after = jnp.where(lane == 127, jnp.where(sec == 0, halo, 0.0), pltpu.roll(plane, 127, 1))
    return 0.5 * (after - before)


def pack_kernel(rho, rest, wave, x_low, x_high, y_low, y_high, z_face):
    high = lax.axis_index("sec") == 0
    for target, plane, wave_plane in ((x_low, 0, 0), (x_high, 15, 7)):
        target[0:32] = rho[plane * 32 : plane * 32 + 32]
        for part in range(4):
            at = part * 512 + plane * 32
            target[32 * part + 32 : 32 * part + 64] = rest[at : at + 32]
            at = part * 128 + wave_plane * 16
            target[160 + 16 * part : 176 + 16 * part] = wave[at : at + 16]
    for target, line, wave_line in ((y_low, 0, 0), (y_high, 31, 15)):
        target[0:16] = rho[pl.ds(line, 16, stride=32)]
        for part in range(4):
            target[16 * part + 16 : 16 * part + 32] = rest[pl.ds(part * 512 + line, 16, stride=32)]
        target[80:88] = wave[pl.ds(wave_line, 8, stride=16)]
        target[88:96] = wave[pl.ds(256 + wave_line, 8, stride=16)]
    eye = iota((128, 128), 0) == iota((128, 128), 1)
    for piece in range(4):
        z_face[piece : piece + 1] = edge_line(rho[piece * 128 : piece * 128 + 128], high, eye)
    for piece in range(16):
        z_face[piece + 4 : piece + 5] = edge_line(rest[piece * 128 : piece * 128 + 128], high, eye)
    z_face[20:21] = edge_line(wave[0:128], high, eye)
    z_face[21:22] = edge_line(wave[384:512], high, eye)
    z_face[22:24] = jnp.zeros((2, 128), F32)


def slot_kernel(owner, counts, patch, slots, valid, patches):
    below = iota((128, 128), 0) < iota((128, 128), 1)
    target = iota((128, 128), 0) * 16
    lane = iota((128, 128), 1)
    lines = [owner[piece : piece + 1].astype(F32) for piece in range(4)]
    columns = [as_column(line) for line in lines]
    for piece in range(4):
        rank = jnp.zeros((1, 128), F32)
        for other in range(piece + 1):
            same = columns[other] == lines[piece]
            if other == piece:
                same = same & below
            rank = rank + jnp.sum(same.astype(F32), axis=0, keepdims=True)
        code = (lines[piece] * 16.0 + rank).astype(jnp.int32)
        here = slice(piece * 128, piece * 128 + 128)
        for slot in range(CAP):
            hit = (target + slot) == code
            slots[slot * 128 : slot * 128 + 128, here] = hit.astype(F32).astype(BF16)
        limit = as_column(counts[piece : piece + 1].astype(F32))
        valid[here] = (lane.astype(F32) < limit).astype(F32)
        patches[here] = as_column(patch[piece : piece + 1].astype(F32)).astype(BF16)


def send_kernel(
    rho, momentum, x_low, x_high, y_low, y_high, z_face, slots, valid, patches, weights,
    send, speed, z_speed, payload,
):
    step = pl.program_id(0)
    steps = pl.num_programs(0)
    lines = 512 // steps
    sec = lax.axis_index("sec")

    @pl.when(step == 0)
    def _():
        for part in range(3):
            speed[part, 32:544] = momentum[part * 512 : part * 512 + 512] / rho[...]
            for at, face in ((0, x_low), (544, x_high)):
                speed[part, at : at + 32] = (
                    face[32 * part + 32 : 32 * part + 64] / safe(face[0:32])
                )
        for part in range(2):
            edge = z_face[4 * part + 4 : 4 * part + 8] / safe(z_face[0:4])
            for piece in range(4):
                z_speed[part, piece * 128 : piece * 128 + 128] = as_column(
                    edge[piece : piece + 1]
                )
        payload[:, 384:512] = patches[...]

    group = iota((16, 128), 0)
    half = iota((16, 128), 1) < 64
    keep = [(group // 4 == part).astype(F32).astype(BF16) for part in range(4)]
    wide = iota((16, 256), 1) // 64 == iota((16, 256), 0) % 4

    for plane in range(lines // 32):
        x = step * (lines // 32) + plane
        at = pl.multiple_of(x * 32, 32)
        v = [speed[part, pl.ds(at + 32, 32)] for part in range(3)]
        v_before = [speed[part, pl.ds(at, 32)] for part in range(3)]
        v_after = [speed[part, pl.ds(at + 64, 32)] for part in range(3)]
        y_before, y_after = {}, {}
        for part in (0, 2):
            here = 16 * part + 16
            y_before[part] = y_low[pl.ds(here + x, 1)] / safe(y_low[pl.ds(x, 1)])
            y_after[part] = y_high[pl.ds(here + x, 1)] / safe(y_high[pl.ds(x, 1)])
        along = {part: 0.5 * (v_after[part] - v_before[part]) for part in (1, 2)}
        across = {
            part: 0.5 * (up(v[part], y_after[part]) - down(v[part], y_before[part]))
            for part in (0, 2)
        }
        deep = {part: derive_z(v[part], z_speed[part, pl.ds(at, 32)], sec) for part in (0, 1)}
        swirl_x = across[2] - deep[1]
        swirl_y = deep[0] - along[2]
        swirl_z = along[1] - across[0]
        mask = valid[pl.ds(at, 32)]
        lamb = [
            ((swirl_y * v[2] - swirl_z * v[1]) * mask).astype(BF16),
            ((swirl_z * v[0] - swirl_x * v[2]) * mask).astype(BF16),
            ((swirl_x * v[1] - swirl_y * v[0]) * mask).astype(BF16),
        ]
        for part in range(2):
            rows = slice(part * 16, part * 16 + 16)
            left = jnp.concatenate(
                [
                    jnp.concatenate([lamb[c][rows] * keep[k] for k in range(4)], axis=1)
                    for c in range(3)
                ],
                axis=0,
            )
            first = plane * 32 + part * 16
            right = jnp.concatenate(
                [
                    weights[(first + 4 * k) * 64 : (first + 4 * k + 4) * 64]
                    for k in range(4)
                ],
                axis=1,
            )
            product = lax.dot_general(
                left, right, (((1,), (1,)), ((), ())), preferred_element_type=F32
            )
            folded = []
            for c in range(3):
                picked = jnp.where(wide, product[c * 16 : c * 16 + 16], 0.0)
                both = picked[:, 0:128] + picked[:, 128:256]
                folded.append(both + pltpu.roll(both, 64, 1))
            pair = jnp.where(half, folded[0], folded[1])
            pair_top = pair.astype(BF16)
            pair_rest = (pair - pair_top.astype(F32)).astype(BF16)
            single_top = folded[2].astype(BF16).astype(F32)
            single = jnp.where(half, single_top, folded[2] - single_top).astype(BF16)
            here = pl.ds(pl.multiple_of(at + part * 16, 16), 16)
            payload[here, 0:128] = pair_top
            payload[here, 128:256] = pair_rest
            payload[here, 256:384] = single

    @pl.when(step == steps - 1)
    def _():
        lane = iota((128, 128), 1)
        numbers = jnp.zeros((128, 128), F32)
        kept = None
        for slot in range(CAP):
            placed = jnp.dot(
                slots[slot * 128 : slot * 128 + 128], payload[...], preferred_element_type=F32
            )
            send[pl.ds(slot, 128, stride=ROWS)] = placed[:, 0:128] + placed[:, 128:256]
            third = placed[:, 256:384]
            third = third + pltpu.roll(third, 64, 1)
            if slot % 2 == 0:
                kept = third
            else:
                send[pl.ds(CAP + slot // 2, 128, stride=ROWS)] = jnp.where(
                    lane < 64, kept, third
                )
            numbers = jnp.where(lane == slot, placed[:, 384:512], numbers)
        send[pl.ds(ROWS - 1, 128, stride=ROWS)] = numbers


def wave_kernel(
    tile_class, wave, x_low, x_high, y_low, y_high, z_face, samples, far, base, share
):
    sec = lax.axis_index("sec")
    level = tile_class[0, 0].astype(F32)
    mean_flow = 0.1 + 0.3 * level
    stiffness = 1.0 + 0.25 * level
    z_pressure = as_column(z_face[20:21])
    z_speed = as_column(z_face[21:22])
    for x in range(8):
        def row(part, at):
            start = part * 128 + at * 16
            if at < 0:
                return x_low[160 + 16 * part : 176 + 16 * part]
            if at > 7:
                return x_high[160 + 16 * part : 176 + 16 * part]
            return wave[start : start + 16]

        now = [row(part, x) for part in range(4)]
        along = [0.5 * (row(part, x + 1) - row(part, x - 1)) for part in range(4)]
        across = [
            0.5
            * (
                up(now[part], y_high[80 + 8 * k + x : 81 + 8 * k + x])
                - down(now[part], y_low[80 + 8 * k + x : 81 + 8 * k + x])
            )
            for k, part in enumerate((0, 2))
        ]
        here = slice(x * 16, x * 16 + 16)
        deep = [derive_z(now[0], z_pressure[here], sec), derive_z(now[3], z_speed[here], sec)]
        divergence = along[1] + across[1] + deep[1]
        base[here] = now[0] - WAVE_STEP * (mean_flow * along[0] + stiffness * divergence)
        for part, gradient in ((1, along[0]), (2, across[0]), (3, deep[0])):
            base[part * 128 + x * 16 : part * 128 + x * 16 + 16] = now[part] - WAVE_STEP * (
                mean_flow * along[part] + gradient
            )
    index = samples[...]
    line, cell = index // 128, index % 128
    picks = (iota((128, 128), 0) == line).astype(F32)
    columns = lax.dot_general(
        base[0:128], picks, (((0,), (0,)), ((), ())),
        precision=lax.Precision.HIGHEST, preferred_element_type=F32,
    )
    values = jnp.sum(
        jnp.where(iota((128, 128), 0) == cell, columns, 0.0), axis=0, keepdims=True
    )
    total = lax.dot_general(
        jnp.broadcast_to(values, (8, 128)), far[...], (((1,), (1,)), ((), ())),
        precision=lax.Precision.HIGHEST, preferred_element_type=F32,
    )
    for block in range(share.shape[0] // 8):
        share[block * 8 : block * 8 + 8] = total


def les_kernel(rho, rest, x_low, x_high, y_low, y_high, z_face, out):
    sec = lax.axis_index("sec")
    lane = iota((32, 128), 1)
    z_rho = safe(z_face[0:4])
    z_v = z_face[12:16] / z_rho
    y_low_v = y_low[32:48] / safe(y_low[0:16])
    y_high_v = y_high[32:48] / safe(y_high[0:16])
    x_low_v = x_low[32:64] / safe(x_low[0:32])
    x_high_v = x_high[32:64] / safe(x_high[0:32])
    for part in range(5):
        def state(x):
            if part == 0:
                return rho[x * 32 : x * 32 + 32]
            return rest[part * 512 - 512 + x * 32 : part * 512 - 512 + x * 32 + 32]

        z_flux = z_face[4 * part : 4 * part + 4] * z_v
        y_low_flux = y_low[16 * part : 16 * part + 16] * y_low_v
        y_high_flux = y_high[16 * part : 16 * part + 16] * y_high_v
        for x in range(16):
            density = rho[x * 32 : x * 32 + 32]
            now = state(x)

            def stream(at):
                if at < 0:
                    return x_low[32 * part : 32 * part + 32] * x_low_v
                if at > 15:
                    return x_high[32 * part : 32 * part + 32] * x_high_v
                return state(at) * (rest[at * 32 : at * 32 + 32] / rho[at * 32 : at * 32 + 32])

            along = 0.5 * (stream(x + 1) - stream(x - 1))
            side = now * (rest[512 + x * 32 : 512 + x * 32 + 32] / density)
            across = 0.5 * (
                up(side, y_high_flux[x : x + 1]) - down(side, y_low_flux[x : x + 1])
            )
            depth = now * (rest[1024 + x * 32 : 1024 + x * 32 + 32] / density)
            if x % 4 == 0:
                z_column = as_column(z_flux[x // 4 : x // 4 + 1])
            deep = derive_z(depth, z_column[x % 4 * 32 : x % 4 * 32 + 32], sec)
            start = part * 512 + x * 32
            out[start : start + 32] = now - LES_STEP * (along + across + deep)


def finish_kernel(arrived, base, shares, out, far):
    names = jnp.transpose(arrived[pl.ds(ROWS - 1, 128, stride=ROWS)])
    place = iota((256, 128), 0)
    patch = (place % 128 * 2 + place // 128).astype(F32)
    half = iota((128, 128), 1) < 64
    total = jnp.zeros((256, 512), F32)
    for pair in range(CAP // 2):
        third = arrived[pl.ds(CAP + pair, 128, stride=ROWS)]
        left, right = [], []
        for slot in (2 * pair, 2 * pair + 1):
            left.append((patch == names[slot : slot + 1]).astype(F32).astype(BF16))
            both = arrived[pl.ds(slot, 128, stride=ROWS)]
            one = jnp.where(half == (slot % 2 == 0), third, 0.0)
            row = []
            for value in (both, one):
                top = value.astype(BF16)
                row += [top, (value - top.astype(F32)).astype(BF16)]
            right.append(jnp.concatenate(row, axis=1))
        total = total + jnp.dot(
            jnp.concatenate(left, axis=1),
            jnp.concatenate(right, axis=0),
            preferred_element_type=F32,
        )
    both = total[:, 0:128] + total[:, 128:256]
    third = total[:, 256:384] + total[:, 384:512]
    third = third + pltpu.roll(third, 64, 1)
    even, odd = both[0:128], both[128:256]
    source = [
        jnp.where(half, even, pltpu.roll(odd, 64, 1)),
        jnp.where(half, pltpu.roll(even, 64, 1), odd),
        jnp.where(half, third[0:128], third[128:256]),
    ]
    out[0:128] = base[0:128]
    for part in range(3):
        here = slice(part * 128 + 128, part * 128 + 256)
        out[here] = base[here] - WAVE_STEP * source[part]
    far[...] = jnp.sum(shares[...], axis=0, keepdims=True)


def call(kernel, outs, flops, moved, limit=16, **more):
    return pl.pallas_call(
        kernel,
        out_shape=[jax.ShapeDtypeStruct(shape, kind) for shape, kind in outs],
        compiler_params=pltpu.CompilerParams(vmem_limit_bytes=limit * MIB),
        cost_estimate=pl.CostEstimate(flops=flops, bytes_accessed=moved, transcendentals=0),
        **more,
    )


def shift(face, axis, offset):
    count = lax.axis_size(axis)
    pairs = [(i, i + offset) for i in range(count) if 0 <= i + offset < count]
    return lax.ppermute(face, axis, pairs)


def per_device(
    les_density,
    les_rest,
    acoustic,
    block_owner,
    block_weights,
    block_counts,
    block_patch,
    tile_class,
    sample_index,
    far_kernel,
):
    rho = les_density.reshape(512, 128)
    rest = les_rest.reshape(2048, 128)
    wave = acoustic.reshape(512, 128)
    with jax.named_scope("pack"):
        faces = call(
            pack_kernel,
            [((224, 128), F32)] * 2 + [((96, 128), F32)] * 2 + [((24, 128), F32)],
            1 << 20, 2 << 20,
        )(rho, rest, wave)
    halos = [
        shift(faces[1], "gx", 1),
        shift(faces[0], "gx", -1),
        shift(faces[3], "row", 1),
        shift(faces[2], "row", -1),
        lax.ppermute(faces[4], "sec", [(0, 1), (1, 0)]),
    ]
    with jax.named_scope("slots"):
        slots, valid, patches = call(
            slot_kernel,
            [((CAP * 128, 512), BF16), ((512, 128), F32), ((512, 128), BF16)],
            1 << 22, 2 << 20,
        )(
            block_owner.reshape(4, 128),
            block_counts.reshape(4, 128),
            block_patch.reshape(4, 128),
        )
    steps = 4
    with jax.named_scope("send"):
        whole = lambda shape: pl.BlockSpec(shape, lambda i: (0, 0))
        (send,) = call(
            send_kernel,
            [((128 * ROWS, 128), F32)],
            1 << 28, 16 << 20, 32,
            grid=(steps,),
            in_specs=[
                whole((512, 128)), whole((1536, 128)),
                whole((224, 128)), whole((224, 128)), whole((96, 128)), whole((96, 128)),
                whole((24, 128)), whole((CAP * 128, 512)), whole((512, 128)),
                whole((512, 128)),
                pl.BlockSpec((512 * 64 // steps, 128), lambda i: (i, 0)),
            ],
            out_specs=[whole((128 * ROWS, 128))],
            scratch_shapes=[
                pltpu.VMEM((3, 576, 128), F32),
                pltpu.VMEM((2, 512, 128), F32),
                pltpu.VMEM((512, 512), BF16),
            ],
        )(rho, rest, *halos, slots, valid, patches, block_weights.reshape(512 * 64, 128))
    arrived = lax.all_to_all(
        send.reshape(128, ROWS, 128), ("gx", "row"), split_axis=0, concat_axis=0, tiled=True
    )
    with jax.named_scope("wave"):
        smem = pl.BlockSpec(memory_space=pltpu.SMEM)
        vmem = pl.BlockSpec(memory_space=pltpu.VMEM)
        base, share = call(
            wave_kernel,
            [((512, 128), F32), ((256, 128), F32)],
            1 << 24, 2 << 20,
            in_specs=[smem] + [vmem] * 8,
        )(
            tile_class.reshape(1, 1), wave, *halos, sample_index.reshape(1, 128), far_kernel
        )
    shares = lax.all_to_all(
        share.reshape(256, 1, 128), ALL, split_axis=0, concat_axis=0, tiled=True
    )
    with jax.named_scope("les"):
        (les_next,) = call(les_kernel, [((2560, 128), F32)], 1 << 23, 4 << 20)(rho, rest, *halos)
    with jax.named_scope("finish"):
        wave_next, far_field = call(
            finish_kernel, [((512, 128), F32), ((1, 128), F32)], 1 << 28, 3 << 20,
        )(arrived.reshape(128 * ROWS, 128), base, shares.reshape(256, 128))
    return (
        les_next.reshape(5, 16, 32, 128),
        wave_next.reshape(4, 8, 16, 128),
        far_field.reshape(128),
    )


def solution(mesh):
    in_specs = (
        P("gx", "row", "sec"),
        P(None, "gx", "row", "sec"),
        P(None, "gx", "row", "sec"),
        P(("sec", "gx", "row"), None),
        P(("sec", "gx", "row"), None, None),
        P(("sec", "gx", "row")),
        P(("sec", "gx", "row")),
        P("sec", "gx", "row"),
        P(("sec", "gx", "row")),
        P(None, ("sec", "gx", "row")),
    )
    out_specs = (P(None, "gx", "row", "sec"), P(None, "gx", "row", "sec"), P())
    return jax.shard_map(
        per_device, mesh=mesh, in_specs=in_specs, out_specs=out_specs, check_vma=False
    )
```

```python
import jax
import jax.numpy as jnp
from jax import lax
from jax.experimental import pallas as pl
from jax.experimental.pallas import tpu as pltpu
from jax.sharding import PartitionSpec as P

LES_STEP = 0.2
WAVE_STEP = 0.25
CAP = 10
ROWS = 17
F32 = jnp.float32
BF16 = jnp.bfloat16
ALL = ("sec", "gx", "row")
MIB = 1 << 20


def iota(shape, dim):
    return lax.broadcasted_iota(jnp.int32, shape, dim)


def as_column(line):
    return jnp.transpose(jnp.broadcast_to(line, (128, 128)))


def edge_line(block, high, eye):
    column = jnp.where(high, block[:, 127:128], block[:, 0:1])
    return jnp.sum(jnp.where(eye, column, 0.0), axis=0, keepdims=True)


def safe(density):
    return jnp.where(density == 0.0, 1.0, density)


def down(plane, halo):
    return jnp.where(iota(plane.shape, 0) == 0, halo, pltpu.roll(plane, 1, 0))


def up(plane, halo):
    last = plane.shape[0] - 1
    return jnp.where(iota(plane.shape, 0) == last, halo, pltpu.roll(plane, last, 0))


def derive_z(plane, halo, sec):
    lane = iota(plane.shape, 1)
    before = jnp.where(lane == 0, jnp.where(sec == 1, halo, 0.0), pltpu.roll(plane, 1, 1))
    after = jnp.where(lane == 127, jnp.where(sec == 0, halo, 0.0), pltpu.roll(plane, 127, 1))
    return 0.5 * (after - before)


def even(axis):
    return lax.rem(lax.axis_index(axis), 2) == 0


def pack_kernel(
    rho_hbm, rest_hbm, wave_hbm, x_even, x_odd, y_even, y_odd, z_face, rho, rest, wave, landed
):
    copies = [
        pltpu.make_async_copy(rho_hbm, rho, landed.at[0]),
        pltpu.make_async_copy(rest_hbm, rest, landed.at[1]),
        pltpu.make_async_copy(wave_hbm, wave, landed.at[2]),
    ]
    for copy in copies:
        copy.start()
    high = lax.axis_index("sec") == 0
    x_index, y_index = even("gx"), even("row")
    eye = iota((128, 128), 0) == iota((128, 128), 1)
    copies[0].wait()
    for piece in range(4):
        z_face[piece : piece + 1] = edge_line(rho[piece * 128 : piece * 128 + 128], high, eye)
    copies[2].wait()
    z_face[20:21] = edge_line(wave[0:128], high, eye)
    z_face[21:22] = edge_line(wave[384:512], high, eye)
    z_face[22:24] = jnp.zeros((2, 128), F32)
    copies[1].wait()
    for piece in range(16):
        z_face[piece + 4 : piece + 5] = edge_line(rest[piece * 128 : piece * 128 + 128], high, eye)
    for target, upper in ((x_even, x_index), (x_odd, jnp.logical_not(x_index))):
        at = pl.multiple_of(jnp.where(upper, 480, 0), 32)
        wave_at = pl.multiple_of(jnp.where(upper, 112, 0), 16)
        target[0:32] = rho[pl.ds(at, 32)]
        for part in range(4):
            target[32 * part + 32 : 32 * part + 64] = rest[pl.ds(part * 512 + at, 32)]
            target[160 + 16 * part : 176 + 16 * part] = wave[pl.ds(part * 128 + wave_at, 16)]
    for target, upper in ((y_even, y_index), (y_odd, jnp.logical_not(y_index))):
        def pick(ref, start, count, width):
            low = ref[pl.ds(start, count, stride=width)]
            return jnp.where(upper, ref[pl.ds(start + width - 1, count, stride=width)], low)

        target[0:16] = pick(rho, 0, 16, 32)
        for part in range(4):
            target[16 * part + 16 : 16 * part + 32] = pick(rest, part * 512, 16, 32)
        target[80:88] = pick(wave, 0, 8, 16)
        target[88:96] = pick(wave, 256, 8, 16)


def sides(x_even, x_odd, y_even, y_odd):
    x_index, y_index = even("gx"), even("row")
    return (
        jnp.where(x_index, x_odd[...], x_even[...]),
        jnp.where(x_index, x_even[...], x_odd[...]),
        jnp.where(y_index, y_odd[...], y_even[...]),
        jnp.where(y_index, y_even[...], y_odd[...]),
    )


def slot_kernel(owner, counts, patch, slots, valid, patches):
    below = iota((128, 128), 0) < iota((128, 128), 1)
    target = iota((128, 128), 0) * 16
    lane = iota((128, 128), 1)
    lines = [owner[piece : piece + 1].astype(F32) for piece in range(4)]
    columns = [as_column(line) for line in lines]
    for piece in range(4):
        rank = jnp.zeros((1, 128), F32)
        for other in range(piece + 1):
            same = columns[other] == lines[piece]
            if other == piece:
                same = same & below
            rank = rank + jnp.sum(same.astype(F32), axis=0, keepdims=True)
        code = (lines[piece] * 16.0 + rank).astype(jnp.int32)
        here = slice(piece * 128, piece * 128 + 128)
        for slot in range(CAP):
            hit = (target + slot) == code
            slots[slot * 128 : slot * 128 + 128, here] = hit.astype(F32).astype(BF16)
        limit = as_column(counts[piece : piece + 1].astype(F32))
        valid[here] = (lane.astype(F32) < limit).astype(F32)
        patches[here] = as_column(patch[piece : piece + 1].astype(F32)).astype(BF16)


def payload_kernel(
    rho, momentum, x_even, x_odd, y_even, y_odd, z_face, valid, weights,
    payload, speed, z_speed, y_speed, held, landed,
):
    steps = landed.shape[0]
    lines = 512 // steps
    sec = lax.axis_index("sec")

    def fetch(step):
        rows = pl.ds(pl.multiple_of(step * (lines * 64), 64), lines * 64)
        return pltpu.make_async_copy(weights.at[rows], held.at[rows], landed.at[step])

    for step in range(steps):
        fetch(step).start()
    x_low, x_high, y_low, y_high = sides(x_even, x_odd, y_even, y_odd)
    for side, face in enumerate((y_low, y_high)):
        for k, part in enumerate((0, 2)):
            y_speed[2 * side + k] = face[16 * part + 16 : 16 * part + 32] / safe(face[0:16])
    for part in range(3):
        speed[part, 32:544] = momentum[part * 512 : part * 512 + 512] / rho[...]
        for at, face in ((0, x_low), (544, x_high)):
            speed[part, at : at + 32] = (
                face[32 * part + 32 : 32 * part + 64] / safe(face[0:32])
            )
    for part in range(2):
        edge = z_face[4 * part + 4 : 4 * part + 8] / safe(z_face[0:4])
        for piece in range(4):
            z_speed[part, piece * 128 : piece * 128 + 128] = as_column(edge[piece : piece + 1])

    group = iota((16, 128), 0)
    half = iota((16, 128), 1) < 64
    keep = [(group // 4 == part).astype(F32).astype(BF16) for part in range(4)]
    wide = iota((16, 256), 1) // 64 == iota((16, 256), 0) % 4

    @pl.loop(0, steps)
    def _(step):
        fetch(step).wait()
        for plane in range(lines // 32):
            x = step * (lines // 32) + plane
            at = pl.multiple_of(x * 32, 32)
            v = [speed[part, pl.ds(at + 32, 32)] for part in range(3)]
            v_before = [speed[part, pl.ds(at, 32)] for part in range(3)]
            v_after = [speed[part, pl.ds(at + 64, 32)] for part in range(3)]
            y_before = {part: y_speed[part // 2, pl.ds(x, 1)] for part in (0, 2)}
            y_after = {part: y_speed[2 + part // 2, pl.ds(x, 1)] for part in (0, 2)}
            along = {part: 0.5 * (v_after[part] - v_before[part]) for part in (1, 2)}
            across = {
                part: 0.5 * (up(v[part], y_after[part]) - down(v[part], y_before[part]))
                for part in (0, 2)
            }
            deep = {part: derive_z(v[part], z_speed[part, pl.ds(at, 32)], sec) for part in (0, 1)}
            swirl_x = across[2] - deep[1]
            swirl_y = deep[0] - along[2]
            swirl_z = along[1] - across[0]
            mask = valid[pl.ds(at, 32)]
            lamb = [
                ((swirl_y * v[2] - swirl_z * v[1]) * mask).astype(BF16),
                ((swirl_z * v[0] - swirl_x * v[2]) * mask).astype(BF16),
                ((swirl_x * v[1] - swirl_y * v[0]) * mask).astype(BF16),
            ]
            for part in range(2):
                rows = slice(part * 16, part * 16 + 16)
                left = jnp.concatenate(
                    [
                        jnp.concatenate([lamb[c][rows] * keep[k] for k in range(4)], axis=1)
                        for c in range(3)
                    ],
                    axis=0,
                )
                first = (x * 32 + part * 16) * 64
                right = jnp.concatenate(
                    [
                        held[pl.ds(pl.multiple_of(first + 256 * k, 256), 256)]
                        for k in range(4)
                    ],
                    axis=1,
                )
                product = lax.dot_general(
                    left, right, (((1,), (1,)), ((), ())), preferred_element_type=F32
                )
                folded = []
                for c in range(3):
                    picked = jnp.where(wide, product[c * 16 : c * 16 + 16], 0.0)
                    both = picked[:, 0:128] + picked[:, 128:256]
                    folded.append(both + pltpu.roll(both, 64, 1))
                pair = jnp.where(half, folded[0], folded[1])
                pair_top = pair.astype(BF16)
                pair_rest = (pair - pair_top.astype(F32)).astype(BF16)
                single_top = folded[2].astype(BF16).astype(F32)
                single = jnp.where(half, single_top, folded[2] - single_top).astype(BF16)
                here = pl.ds(pl.multiple_of(at + part * 16, 16), 16)
                payload[here, 0:128] = pair_top
                payload[here, 128:256] = pair_rest
                payload[here, 256:384] = single


def place_kernel(slots, payload, patches, share, other, send):
    lane = iota((128, 128), 1)
    numbers = jnp.zeros((128, 128), F32)
    kept = None
    values = jnp.concatenate([payload[...], patches[...]], axis=1)
    for slot in range(CAP):
        placed = jnp.dot(
            slots[slot * 128 : slot * 128 + 128], values, preferred_element_type=F32
        )
        send[pl.ds(slot, 128, stride=ROWS)] = placed[:, 0:128] + placed[:, 128:256]
        third = placed[:, 256:384]
        third = third + pltpu.roll(third, 64, 1)
        if slot % 2 == 0:
            kept = third
        else:
            send[pl.ds(CAP + slot // 2, 128, stride=ROWS)] = jnp.where(lane < 64, kept, third)
        numbers = jnp.where(lane == slot, placed[:, 384:512], numbers)
    send[pl.ds(CAP * 3 // 2, 128, stride=ROWS)] = numbers
    both = share[0:1] + other[0:1]
    send[pl.ds(CAP * 3 // 2 + 1, 128, stride=ROWS)] = jnp.broadcast_to(both, (128, 128))


def wave_kernel(
    tile_class, wave, x_even, x_odd, y_even, y_odd, z_face, samples, far, base, share
):
    sec = lax.axis_index("sec")
    x_low, x_high, y_low, y_high = sides(x_even, x_odd, y_even, y_odd)
    level = tile_class[0, 0].astype(F32)
    mean_flow = 0.1 + 0.3 * level
    stiffness = 1.0 + 0.25 * level
    z_pressure = as_column(z_face[20:21])
    z_speed = as_column(z_face[21:22])
    for x in range(8):
        def row(part, at):
            start = part * 128 + at * 16
            if at < 0:
                return x_low[160 + 16 * part : 176 + 16 * part]
            if at > 7:
                return x_high[160 + 16 * part : 176 + 16 * part]
            return wave[start : start + 16]

        now = [row(part, x) for part in range(4)]
        along = [0.5 * (row(part, x + 1) - row(part, x - 1)) for part in range(4)]
        across = [
            0.5
            * (
                up(now[part], y_high[80 + 8 * k + x : 81 + 8 * k + x])
                - down(now[part], y_low[80 + 8 * k + x : 81 + 8 * k + x])
            )
            for k, part in enumerate((0, 2))
        ]
        here = slice(x * 16, x * 16 + 16)
        deep = [derive_z(now[0], z_pressure[here], sec), derive_z(now[3], z_speed[here], sec)]
        divergence = along[1] + across[1] + deep[1]
        base[here] = now[0] - WAVE_STEP * (mean_flow * along[0] + stiffness * divergence)
        for part, gradient in ((1, along[0]), (2, across[0]), (3, deep[0])):
            base[part * 128 + x * 16 : part * 128 + x * 16 + 16] = now[part] - WAVE_STEP * (
                mean_flow * along[part] + gradient
            )
    index = samples[...]
    line, cell = index // 128, index % 128
    picks = (iota((128, 128), 0) == line).astype(F32)
    columns = lax.dot_general(
        base[0:128], picks, (((0,), (0,)), ((), ())),
        precision=lax.Precision.HIGHEST, preferred_element_type=F32,
    )
    values = jnp.sum(
        jnp.where(iota((128, 128), 0) == cell, columns, 0.0), axis=0, keepdims=True
    )
    share[...] = lax.dot_general(
        jnp.broadcast_to(values, (8, 128)), far[...], (((1,), (1,)), ((), ())),
        precision=lax.Precision.HIGHEST, preferred_element_type=F32,
    )


def les_kernel(rho, rest, x_even, x_odd, y_even, y_odd, z_face, out):
    sec = lax.axis_index("sec")
    x_low, x_high, y_low, y_high = sides(x_even, x_odd, y_even, y_odd)
    lane = iota((32, 128), 1)
    z_rho = safe(z_face[0:4])
    z_v = z_face[12:16] / z_rho
    y_low_v = y_low[32:48] / safe(y_low[0:16])
    y_high_v = y_high[32:48] / safe(y_high[0:16])
    x_low_v = x_low[32:64] / safe(x_low[0:32])
    x_high_v = x_high[32:64] / safe(x_high[0:32])
    for part in range(5):
        def state(x):
            if part == 0:
                return rho[x * 32 : x * 32 + 32]
            return rest[part * 512 - 512 + x * 32 : part * 512 - 512 + x * 32 + 32]

        z_flux = z_face[4 * part : 4 * part + 4] * z_v
        y_low_flux = y_low[16 * part : 16 * part + 16] * y_low_v
        y_high_flux = y_high[16 * part : 16 * part + 16] * y_high_v
        for x in range(16):
            density = rho[x * 32 : x * 32 + 32]
            now = state(x)

            def stream(at):
                if at < 0:
                    return x_low[32 * part : 32 * part + 32] * x_low_v
                if at > 15:
                    return x_high[32 * part : 32 * part + 32] * x_high_v
                return state(at) * (rest[at * 32 : at * 32 + 32] / rho[at * 32 : at * 32 + 32])

            along = 0.5 * (stream(x + 1) - stream(x - 1))
            side = now * (rest[512 + x * 32 : 512 + x * 32 + 32] / density)
            across = 0.5 * (
                up(side, y_high_flux[x : x + 1]) - down(side, y_low_flux[x : x + 1])
            )
            depth = now * (rest[1024 + x * 32 : 1024 + x * 32 + 32] / density)
            if x % 4 == 0:
                z_column = as_column(z_flux[x // 4 : x // 4 + 1])
            deep = derive_z(depth, z_column[x % 4 * 32 : x % 4 * 32 + 32], sec)
            start = part * 512 + x * 32
            out[start : start + 32] = now - LES_STEP * (along + across + deep)


def finish_kernel(arrived, base, out, far):
    names = jnp.transpose(arrived[pl.ds(CAP * 3 // 2, 128, stride=ROWS)])
    place = iota((256, 128), 0)
    patch = (place % 128 * 2 + place // 128).astype(F32)
    half = iota((128, 128), 1) < 64
    total = jnp.zeros((256, 512), F32)
    for pair in range(CAP // 2):
        third = arrived[pl.ds(CAP + pair, 128, stride=ROWS)]
        left, right = [], []
        for slot in (2 * pair, 2 * pair + 1):
            left.append((patch == names[slot : slot + 1]).astype(F32).astype(BF16))
            both = arrived[pl.ds(slot, 128, stride=ROWS)]
            one = jnp.where(half == (slot % 2 == 0), third, 0.0)
            row = []
            for value in (both, one):
                top = value.astype(BF16)
                row += [top, (value - top.astype(F32)).astype(BF16)]
            right.append(jnp.concatenate(row, axis=1))
        total = total + jnp.dot(
            jnp.concatenate(left, axis=1),
            jnp.concatenate(right, axis=0),
            preferred_element_type=F32,
        )
    both = total[:, 0:128] + total[:, 128:256]
    third = total[:, 256:384] + total[:, 384:512]
    third = third + pltpu.roll(third, 64, 1)
    even, odd = both[0:128], both[128:256]
    source = [
        jnp.where(half, even, pltpu.roll(odd, 64, 1)),
        jnp.where(half, pltpu.roll(even, 64, 1), odd),
        jnp.where(half, third[0:128], third[128:256]),
    ]
    out[0:128] = base[0:128]
    for part in range(3):
        here = slice(part * 128 + 128, part * 128 + 256)
        out[here] = base[here] - WAVE_STEP * source[part]
    shares = arrived[pl.ds(CAP * 3 // 2 + 1, 128, stride=ROWS)]
    far[...] = jnp.sum(shares, axis=0, keepdims=True)


def call(kernel, outs, flops, moved, limit=16, **more):
    return pl.pallas_call(
        kernel,
        out_shape=[jax.ShapeDtypeStruct(shape, kind) for shape, kind in outs],
        compiler_params=pltpu.CompilerParams(vmem_limit_bytes=limit * MIB),
        cost_estimate=pl.CostEstimate(flops=flops, bytes_accessed=moved, transcendentals=0),
        **more,
    )


def exchange(face, axis, first):
    pairs = []
    for low in range(first, lax.axis_size(axis) - 1, 2):
        pairs += [(low, low + 1), (low + 1, low)]
    return lax.ppermute(face, axis, pairs)


def per_device(
    les_density,
    les_rest,
    acoustic,
    block_owner,
    block_weights,
    block_counts,
    block_patch,
    tile_class,
    sample_index,
    far_kernel,
):
    rho = les_density.reshape(512, 128)
    rest = les_rest.reshape(2048, 128)
    wave = acoustic.reshape(512, 128)
    weights = block_weights.reshape(512 * 64, 128)
    hbm = pl.BlockSpec(memory_space=pltpu.HBM)
    vmem = pl.BlockSpec(memory_space=pltpu.VMEM)
    smem = pl.BlockSpec(memory_space=pltpu.SMEM)
    pinned = lambda x: pltpu.with_memory_space_constraint(x, pltpu.HBM)
    with jax.named_scope("pack"):
        faces = call(
            pack_kernel,
            [((224, 128), F32)] * 2 + [((96, 128), F32)] * 2 + [((24, 128), F32)],
            1 << 20, 2 << 20,
            in_specs=[hbm] * 3,
            scratch_shapes=[
                pltpu.VMEM((512, 128), F32),
                pltpu.VMEM((2048, 128), F32),
                pltpu.VMEM((512, 128), F32),
                pltpu.SemaphoreType.DMA((3,)),
            ],
        )(pinned(rho), pinned(rest), pinned(wave))
    halos = [
        exchange(faces[0], "gx", 0),
        exchange(faces[1], "gx", 1),
        exchange(faces[2], "row", 0),
        exchange(faces[3], "row", 1),
        exchange(faces[4], "sec", 0),
    ]
    with jax.named_scope("slots"):
        slots, valid, patches = call(
            slot_kernel,
            [((CAP * 128, 512), BF16), ((512, 128), F32), ((512, 128), BF16)],
            1 << 22, 2 << 20,
        )(
            block_owner.reshape(4, 128),
            block_counts.reshape(4, 128),
            block_patch.reshape(4, 128),
        )
    with jax.named_scope("wave"):
        base, share = call(
            wave_kernel,
            [((512, 128), F32), ((8, 128), F32)],
            1 << 24, 2 << 20,
            in_specs=[smem] + [vmem] * 8,
        )(
            tile_class.reshape(1, 1), wave, *halos, sample_index.reshape(1, 128), far_kernel
        )
    other = exchange(share, "sec", 0)
    with jax.named_scope("payload"):
        (payload,) = call(
            payload_kernel,
            [((512, 384), BF16)],
            1 << 27, 16 << 20, 32,
            in_specs=[vmem] * 8 + [hbm],
            scratch_shapes=[
                pltpu.VMEM((3, 576, 128), F32),
                pltpu.VMEM((2, 512, 128), F32),
                pltpu.VMEM((4, 16, 128), F32),
                pltpu.VMEM((512 * 64, 128), BF16),
                pltpu.SemaphoreType.DMA((4,)),
            ],
        )(rho, rest, *halos, valid, pinned(weights))
    with jax.named_scope("place"):
        (send,) = call(place_kernel, [((128 * ROWS, 128), F32)], 1 << 28, 3 << 20)(
            slots, payload, patches, share, other
        )
    arrived = lax.all_to_all(
        send.reshape(128, 1, ROWS * 128), ("gx", "row"), split_axis=0, concat_axis=0, tiled=True
    )
    with jax.named_scope("les"):
        (les_next,) = call(les_kernel, [((2560, 128), F32)], 1 << 23, 4 << 20)(rho, rest, *halos)
    with jax.named_scope("finish"):
        wave_next, far_field = call(
            finish_kernel, [((512, 128), F32), ((1, 128), F32)], 1 << 28, 3 << 20,
        )(arrived.reshape(128 * ROWS, 128), base)
    return (
        les_next.reshape(5, 16, 32, 128),
        wave_next.reshape(4, 8, 16, 128),
        far_field.reshape(128),
    )


def solution(mesh):
    in_specs = (
        P("gx", "row", "sec"),
        P(None, "gx", "row", "sec"),
        P(None, "gx", "row", "sec"),
        P(("sec", "gx", "row"), None),
        P(("sec", "gx", "row"), None, None),
        P(("sec", "gx", "row")),
        P(("sec", "gx", "row")),
        P("sec", "gx", "row"),
        P(("sec", "gx", "row")),
        P(None, ("sec", "gx", "row")),
    )
    out_specs = (P(None, "gx", "row", "sec"), P(None, "gx", "row", "sec"), P())
    return jax.shard_map(
        per_device, mesh=mesh, in_specs=in_specs, out_specs=out_specs, check_vma=False
    )
```

```python
import jax
import jax.numpy as jnp
from jax import lax
from jax.experimental import pallas as pl
from jax.experimental.pallas import tpu as pltpu
from jax.sharding import PartitionSpec as P

LES_STEP = 0.2
WAVE_STEP = 0.25
CAP = 10
ROWS = 17
F32 = jnp.float32
BF16 = jnp.bfloat16
ALL = ("sec", "gx", "row")
MIB = 1 << 20


def iota(shape, dim):
    return lax.broadcasted_iota(jnp.int32, shape, dim)


def as_column(line):
    return jnp.transpose(jnp.broadcast_to(line, (128, 128)))


def edge_line(block, high, eye):
    column = jnp.where(high, block[:, 127:128], block[:, 0:1])
    return jnp.sum(jnp.where(eye, column, 0.0), axis=0, keepdims=True)


def safe(density):
    return jnp.where(density == 0.0, 1.0, density)


def down(plane, halo):
    return jnp.where(iota(plane.shape, 0) == 0, halo, pltpu.roll(plane, 1, 0))


def up(plane, halo):
    last = plane.shape[0] - 1
    return jnp.where(iota(plane.shape, 0) == last, halo, pltpu.roll(plane, last, 0))


def derive_z(plane, halo, sec):
    lane = iota(plane.shape, 1)
    before = jnp.where(lane == 0, jnp.where(sec == 1, halo, 0.0), pltpu.roll(plane, 1, 1))
    after = jnp.where(lane == 127, jnp.where(sec == 0, halo, 0.0), pltpu.roll(plane, 127, 1))
    return 0.5 * (after - before)


def even(axis):
    return lax.rem(lax.axis_index(axis), 2) == 0


def pack_kernel(
    rho_hbm, rest_hbm, wave_hbm, far, x_even, x_odd, y_even, y_odd, z_face, rho, rest, wave, landed
):
    copies = [pltpu.make_async_copy(rho_hbm, rho, landed.at[0])]
    for part in range(4):
        rows = pl.ds(part * 512, 512)
        copies.append(pltpu.make_async_copy(rest_hbm.at[rows], rest.at[rows], landed.at[part + 1]))
    copies.append(pltpu.make_async_copy(wave_hbm, wave, landed.at[5]))
    for copy in copies:
        copy.start()
    high = lax.axis_index("sec") == 0
    x_index, y_index = even("gx"), even("row")
    x_targets = (x_even, x_index), (x_odd, jnp.logical_not(x_index))
    y_targets = (y_even, y_index), (y_odd, jnp.logical_not(y_index))
    eye = iota((128, 128), 0) == iota((128, 128), 1)

    def pick(ref, start, count, width, upper):
        low = ref[pl.ds(start, count, stride=width)]
        return jnp.where(upper, ref[pl.ds(start + width - 1, count, stride=width)], low)

    for field in range(5):
        copies[field].wait()
        ref, first = (rho, 0) if field == 0 else (rest, field * 512 - 512)
        for target, upper in x_targets:
            at = pl.multiple_of(first + jnp.where(upper, 480, 0), 32)
            target[field * 32 : field * 32 + 32] = ref[pl.ds(at, 32)]
        for target, upper in y_targets:
            target[field * 16 : field * 16 + 16] = pick(ref, first, 16, 32, upper)
        for piece in range(4):
            here = first + piece * 128
            line = edge_line(ref[here : here + 128], high, eye)
            z_face[field * 4 + piece : field * 4 + piece + 1] = line
    copies[5].wait()
    for target, upper in x_targets:
        at = pl.multiple_of(jnp.where(upper, 112, 0), 16)
        for part in range(4):
            target[160 + 16 * part : 176 + 16 * part] = wave[pl.ds(part * 128 + at, 16)]
    for target, upper in y_targets:
        target[80:88] = pick(wave, 0, 8, 16, upper)
        target[88:96] = pick(wave, 256, 8, 16, upper)
    z_face[20:21] = edge_line(wave[0:128], high, eye)
    z_face[21:22] = edge_line(wave[384:512], high, eye)
    z_face[22:24] = jnp.zeros((2, 128), F32)


def sides(x_even, x_odd, y_even, y_odd):
    x_index, y_index = even("gx"), even("row")
    return (
        jnp.where(x_index, x_odd[...], x_even[...]),
        jnp.where(x_index, x_even[...], x_odd[...]),
        jnp.where(y_index, y_odd[...], y_even[...]),
        jnp.where(y_index, y_even[...], y_odd[...]),
    )


def slot_kernel(owner, counts, patch, weights, slots, valid, patches):
    below = iota((128, 128), 0) < iota((128, 128), 1)
    target = iota((128, 128), 0) * 16
    lane = iota((128, 128), 1)
    lines = [owner[piece : piece + 1].astype(F32) for piece in range(4)]
    columns = [as_column(line) for line in lines]
    for piece in range(4):
        rank = jnp.zeros((1, 128), F32)
        for other in range(piece + 1):
            same = columns[other] == lines[piece]
            if other == piece:
                same = same & below
            rank = rank + jnp.sum(same.astype(F32), axis=0, keepdims=True)
        code = (lines[piece] * 16.0 + rank).astype(jnp.int32)
        here = slice(piece * 128, piece * 128 + 128)
        for slot in range(CAP):
            hit = (target + slot) == code
            slots[slot * 128 : slot * 128 + 128, here] = hit.astype(F32).astype(BF16)
        limit = as_column(counts[piece : piece + 1].astype(F32))
        valid[here] = (lane.astype(F32) < limit).astype(F32)
        patches[here] = as_column(patch[piece : piece + 1].astype(F32)).astype(BF16)


def payload_kernel(
    rho, momentum, x_even, x_odd, y_even, y_odd, z_face, valid, weights,
    payload, speed, z_speed, y_speed,
):
    sec = lax.axis_index("sec")

    x_low, x_high, y_low, y_high = sides(x_even, x_odd, y_even, y_odd)
    for side, face in enumerate((y_low, y_high)):
        for k, part in enumerate((0, 2)):
            y_speed[2 * side + k] = face[16 * part + 16 : 16 * part + 32] / safe(face[0:16])
    inverse = 1.0 / rho[...]
    for part in range(3):
        speed[part, 32:544] = momentum[part * 512 : part * 512 + 512] * inverse
        for at, face in ((0, x_low), (544, x_high)):
            speed[part, at : at + 32] = (
                face[32 * part + 32 : 32 * part + 64] / safe(face[0:32])
            )
    for part in range(2):
        edge = z_face[4 * part + 4 : 4 * part + 8] / safe(z_face[0:4])
        for piece in range(4):
            z_speed[part, piece * 128 : piece * 128 + 128] = as_column(edge[piece : piece + 1])

    group = iota((16, 128), 0)
    half = iota((16, 128), 1) < 64
    keep = [(group // 4 == part).astype(F32).astype(BF16) for part in range(4)]
    wide = iota((16, 256), 1) // 64 == iota((16, 256), 0) % 4

    for x in range(16):
        at = x * 32
        v = [speed[part, pl.ds(at + 32, 32)] for part in range(3)]
        v_before = [speed[part, pl.ds(at, 32)] for part in range(3)]
        v_after = [speed[part, pl.ds(at + 64, 32)] for part in range(3)]
        y_before = {part: y_speed[part // 2, pl.ds(x, 1)] for part in (0, 2)}
        y_after = {part: y_speed[2 + part // 2, pl.ds(x, 1)] for part in (0, 2)}
        along = {part: 0.5 * (v_after[part] - v_before[part]) for part in (1, 2)}
        across = {
            part: 0.5 * (up(v[part], y_after[part]) - down(v[part], y_before[part]))
            for part in (0, 2)
        }
        deep = {part: derive_z(v[part], z_speed[part, pl.ds(at, 32)], sec) for part in (0, 1)}
        swirl_x = across[2] - deep[1]
        swirl_y = deep[0] - along[2]
        swirl_z = along[1] - across[0]
        mask = valid[pl.ds(at, 32)]
        lamb = [
            ((swirl_y * v[2] - swirl_z * v[1]) * mask).astype(BF16),
            ((swirl_z * v[0] - swirl_x * v[2]) * mask).astype(BF16),
            ((swirl_x * v[1] - swirl_y * v[0]) * mask).astype(BF16),
        ]
        for part in range(2):
            rows = slice(part * 16, part * 16 + 16)
            left = jnp.concatenate(
                [
                    jnp.concatenate([lamb[c][rows] * keep[k] for k in range(4)], axis=1)
                    for c in range(3)
                ],
                axis=0,
            )
            first = (x * 32 + part * 16) * 64
            right = jnp.concatenate(
                [
                    weights[first + 256 * k : first + 256 * k + 256]
                    for k in range(4)
                ],
                axis=1,
            )
            product = lax.dot_general(
                left, right, (((1,), (1,)), ((), ())), preferred_element_type=F32
            )
            folded = []
            for c in range(3):
                picked = jnp.where(wide, product[c * 16 : c * 16 + 16], 0.0)
                both = picked[:, 0:128] + picked[:, 128:256]
                folded.append(both + pltpu.roll(both, 64, 1))
            pair = jnp.where(half, folded[0], folded[1])
            pair_top = pair.astype(BF16)
            pair_rest = (pair - pair_top.astype(F32)).astype(BF16)
            single_top = folded[2].astype(BF16).astype(F32)
            single = jnp.where(half, single_top, folded[2] - single_top).astype(BF16)
            here = slice(at + part * 16, at + part * 16 + 16)
            payload[here, 0:128] = pair_top
            payload[here, 128:256] = pair_rest
            payload[here, 256:384] = single


def place_kernel(slots, payload, patches, share, other, send, rows, sent):
    half = iota((32, 128), 1) < 64
    lane = iota((32, 128), 1)
    values = jnp.concatenate([payload[...], patches[...]], axis=1)
    both = jnp.broadcast_to(share[0:1] + other[0:1], (32, 128))
    copies = []
    for block in range(4):
        hits = [slots[slot * 128 + block * 32 : slot * 128 + block * 32 + 32] for slot in range(CAP)]
        placed = jnp.dot(jnp.concatenate(hits, axis=0), values, preferred_element_type=F32)
        first = block * 32 * ROWS
        numbers = jnp.zeros((32, 128), F32)
        for slot in range(CAP):
            mine = placed[slot * 32 : slot * 32 + 32]
            rows[pl.ds(first + slot, 32, stride=ROWS)] = mine[:, 0:128] + mine[:, 128:256]
            third = mine[:, 256:384]
            third = third + pltpu.roll(third, 64, 1)
            if slot % 2 == 0:
                kept = third
            else:
                rows[pl.ds(first + CAP + slot // 2, 32, stride=ROWS)] = jnp.where(
                    half, kept, third
                )
            numbers = jnp.where(lane == slot, mine[:, 384:512], numbers)
        rows[pl.ds(first + CAP * 3 // 2, 32, stride=ROWS)] = numbers
        rows[pl.ds(first + CAP * 3 // 2 + 1, 32, stride=ROWS)] = both
        here = pl.ds(first, 32 * ROWS)
        copy = pltpu.make_async_copy(rows.at[here], send.at[here], sent.at[block])
        copy.start()
        copies.append(copy)
    for copy in copies:
        copy.wait()


def wave_kernel(
    tile_class, wave, x_even, x_odd, y_even, y_odd, z_face, samples, far, base, share
):
    sec = lax.axis_index("sec")
    x_low, x_high, y_low, y_high = sides(x_even, x_odd, y_even, y_odd)
    level = tile_class[0, 0].astype(F32)
    mean_flow = 0.1 + 0.3 * level
    stiffness = 1.0 + 0.25 * level
    z_pressure = as_column(z_face[20:21])
    z_speed = as_column(z_face[21:22])
    for x in range(8):
        def row(part, at):
            start = part * 128 + at * 16
            if at < 0:
                return x_low[160 + 16 * part : 176 + 16 * part]
            if at > 7:
                return x_high[160 + 16 * part : 176 + 16 * part]
            return wave[start : start + 16]

        now = [row(part, x) for part in range(4)]
        along = [0.5 * (row(part, x + 1) - row(part, x - 1)) for part in range(4)]
        across = [
            0.5
            * (
                up(now[part], y_high[80 + 8 * k + x : 81 + 8 * k + x])
                - down(now[part], y_low[80 + 8 * k + x : 81 + 8 * k + x])
            )
            for k, part in enumerate((0, 2))
        ]
        here = slice(x * 16, x * 16 + 16)
        deep = [derive_z(now[0], z_pressure[here], sec), derive_z(now[3], z_speed[here], sec)]
        divergence = along[1] + across[1] + deep[1]
        base[here] = now[0] - WAVE_STEP * (mean_flow * along[0] + stiffness * divergence)
        for part, gradient in ((1, along[0]), (2, across[0]), (3, deep[0])):
            base[part * 128 + x * 16 : part * 128 + x * 16 + 16] = now[part] - WAVE_STEP * (
                mean_flow * along[part] + gradient
            )
    index = samples[...]
    line, cell = index // 128, index % 128
    picks = (iota((128, 128), 0) == line).astype(F32)
    columns = lax.dot_general(
        base[0:128], picks, (((0,), (0,)), ((), ())),
        precision=lax.Precision.HIGHEST, preferred_element_type=F32,
    )
    values = jnp.sum(
        jnp.where(iota((128, 128), 0) == cell, columns, 0.0), axis=0, keepdims=True
    )
    share[...] = lax.dot_general(
        jnp.broadcast_to(values, (8, 128)), far[...], (((1,), (1,)), ((), ())),
        precision=lax.Precision.HIGHEST, preferred_element_type=F32,
    )


def les_kernel(rho, rest, x_even, x_odd, y_even, y_odd, z_face, out):
    sec = lax.axis_index("sec")
    x_low, x_high, y_low, y_high = sides(x_even, x_odd, y_even, y_odd)
    lane = iota((32, 128), 1)
    z_rho = safe(z_face[0:4])
    z_v = z_face[12:16] / z_rho
    y_low_v = y_low[32:48] / safe(y_low[0:16])
    y_high_v = y_high[32:48] / safe(y_high[0:16])
    x_low_v = x_low[32:64] / safe(x_low[0:32])
    x_high_v = x_high[32:64] / safe(x_high[0:32])
    for part in range(5):
        def state(x):
            if part == 0:
                return rho[x * 32 : x * 32 + 32]
            return rest[part * 512 - 512 + x * 32 : part * 512 - 512 + x * 32 + 32]

        z_flux = z_face[4 * part : 4 * part + 4] * z_v
        y_low_flux = y_low[16 * part : 16 * part + 16] * y_low_v
        y_high_flux = y_high[16 * part : 16 * part + 16] * y_high_v
        for x in range(16):
            density = rho[x * 32 : x * 32 + 32]
            now = state(x)

            def stream(at):
                if at < 0:
                    return x_low[32 * part : 32 * part + 32] * x_low_v
                if at > 15:
                    return x_high[32 * part : 32 * part + 32] * x_high_v
                return state(at) * (rest[at * 32 : at * 32 + 32] / rho[at * 32 : at * 32 + 32])

            along = 0.5 * (stream(x + 1) - stream(x - 1))
            side = now * (rest[512 + x * 32 : 512 + x * 32 + 32] / density)
            across = 0.5 * (
                up(side, y_high_flux[x : x + 1]) - down(side, y_low_flux[x : x + 1])
            )
            depth = now * (rest[1024 + x * 32 : 1024 + x * 32 + 32] / density)
            if x % 4 == 0:
                z_column = as_column(z_flux[x // 4 : x // 4 + 1])
            deep = derive_z(depth, z_column[x % 4 * 32 : x % 4 * 32 + 32], sec)
            start = part * 512 + x * 32
            out[start : start + 32] = now - LES_STEP * (along + across + deep)


def finish_kernel(arrived, base, out, far):
    names = jnp.transpose(arrived[pl.ds(CAP * 3 // 2, 128, stride=ROWS)])
    place = iota((256, 128), 0)
    patch = (place % 128 * 2 + place // 128).astype(F32)
    half = iota((128, 128), 1) < 64
    total = jnp.zeros((256, 512), F32)
    for pair in range(CAP // 2):
        third = arrived[pl.ds(CAP + pair, 128, stride=ROWS)]
        left, right = [], []
        for slot in (2 * pair, 2 * pair + 1):
            left.append((patch == names[slot : slot + 1]).astype(F32).astype(BF16))
            both = arrived[pl.ds(slot, 128, stride=ROWS)]
            one = jnp.where(half == (slot % 2 == 0), third, 0.0)
            row = []
            for value in (both, one):
                top = value.astype(BF16)
                row += [top, (value - top.astype(F32)).astype(BF16)]
            right.append(jnp.concatenate(row, axis=1))
        total = total + jnp.dot(
            jnp.concatenate(left, axis=1),
            jnp.concatenate(right, axis=0),
            preferred_element_type=F32,
        )
    both = total[:, 0:128] + total[:, 128:256]
    third = total[:, 256:384] + total[:, 384:512]
    third = third + pltpu.roll(third, 64, 1)
    even, odd = both[0:128], both[128:256]
    source = [
        jnp.where(half, even, pltpu.roll(odd, 64, 1)),
        jnp.where(half, pltpu.roll(even, 64, 1), odd),
        jnp.where(half, third[0:128], third[128:256]),
    ]
    out[0:128] = base[0:128]
    for part in range(3):
        here = slice(part * 128 + 128, part * 128 + 256)
        out[here] = base[here] - WAVE_STEP * source[part]
    shares = arrived[pl.ds(CAP * 3 // 2 + 1, 128, stride=ROWS)]
    far[...] = jnp.sum(shares, axis=0, keepdims=True)


def call(kernel, outs, flops, moved, limit=16, **more):
    return pl.pallas_call(
        kernel,
        out_shape=[jax.ShapeDtypeStruct(shape, kind) for shape, kind in outs],
        compiler_params=pltpu.CompilerParams(vmem_limit_bytes=limit * MIB),
        cost_estimate=pl.CostEstimate(flops=flops, bytes_accessed=moved, transcendentals=0),
        **more,
    )


def exchange(face, axis, first):
    pairs = []
    for low in range(first, lax.axis_size(axis) - 1, 2):
        pairs += [(low, low + 1), (low + 1, low)]
    return lax.ppermute(face, axis, pairs)


def per_device(
    les_density,
    les_rest,
    acoustic,
    block_owner,
    block_weights,
    block_counts,
    block_patch,
    tile_class,
    sample_index,
    far_kernel,
):
    rho = les_density.reshape(512, 128)
    rest = les_rest.reshape(2048, 128)
    wave = acoustic.reshape(512, 128)
    weights = block_weights.reshape(512 * 64, 128)
    hbm = pl.BlockSpec(memory_space=pltpu.HBM)
    vmem = pl.BlockSpec(memory_space=pltpu.VMEM)
    smem = pl.BlockSpec(memory_space=pltpu.SMEM)
    pinned = lambda x: pltpu.with_memory_space_constraint(x, pltpu.HBM)
    with jax.named_scope("pack"):
        faces = call(
            pack_kernel,
            [((224, 128), F32)] * 2 + [((96, 128), F32)] * 2 + [((24, 128), F32)],
            1 << 20, 2 << 20,
            in_specs=[hbm] * 4,
            scratch_shapes=[
                pltpu.VMEM((512, 128), F32),
                pltpu.VMEM((2048, 128), F32),
                pltpu.VMEM((512, 128), F32),
                pltpu.SemaphoreType.DMA((6,)),
            ],
        )(pinned(rho), pinned(rest), pinned(wave), pinned(far_kernel))
    halos = [
        exchange(faces[0], "gx", 0),
        exchange(faces[1], "gx", 1),
        exchange(faces[2], "row", 0),
        exchange(faces[3], "row", 1),
        exchange(faces[4], "sec", 0),
    ]
    with jax.named_scope("slots"):
        slots, valid, patches = call(
            slot_kernel,
            [((CAP * 128, 512), BF16), ((512, 128), F32), ((512, 128), BF16)],
            1 << 22, 2 << 20,
            in_specs=[vmem] * 3 + [hbm],
        )(
            block_owner.reshape(4, 128),
            block_counts.reshape(4, 128),
            block_patch.reshape(4, 128),
            pinned(weights),
        )
    with jax.named_scope("wave"):
        base, share = call(
            wave_kernel,
            [((512, 128), F32), ((8, 128), F32)],
            1 << 24, 2 << 20,
            in_specs=[smem] + [vmem] * 8,
        )(
            tile_class.reshape(1, 1), wave, *halos, sample_index.reshape(1, 128), far_kernel
        )
    other = exchange(share, "sec", 0)
    with jax.named_scope("payload"):
        (payload,) = call(
            payload_kernel,
            [((512, 384), BF16)],
            1 << 27, 16 << 20, 24,
            in_specs=[vmem] * 9,
            scratch_shapes=[
                pltpu.VMEM((3, 576, 128), F32),
                pltpu.VMEM((2, 512, 128), F32),
                pltpu.VMEM((4, 16, 128), F32),
            ],
        )(rho, rest, *halos, valid, weights)
    with jax.named_scope("place"):
        (send,) = call(
            place_kernel,
            [((128 * ROWS, 128), F32)],
            1 << 28, 3 << 20,
            out_specs=[hbm],
            scratch_shapes=[
                pltpu.VMEM((128 * ROWS, 128), F32),
                pltpu.SemaphoreType.DMA((4,)),
            ],
        )(slots, payload, patches, share, other)
    arrived = lax.all_to_all(
        send.reshape(128, 1, ROWS * 128), ("gx", "row"), split_axis=0, concat_axis=0, tiled=True
    )
    with jax.named_scope("les"):
        (les_next,) = call(les_kernel, [((2560, 128), F32)], 1 << 23, 4 << 20)(rho, rest, *halos)
    with jax.named_scope("finish"):
        wave_next, far_field = call(
            finish_kernel, [((512, 128), F32), ((1, 128), F32)], 1 << 28, 3 << 20,
        )(arrived.reshape(128 * ROWS, 128), base)
    return (
        les_next.reshape(5, 16, 32, 128),
        wave_next.reshape(4, 8, 16, 128),
        far_field.reshape(128),
    )


def solution(mesh):
    in_specs = (
        P("gx", "row", "sec"),
        P(None, "gx", "row", "sec"),
        P(None, "gx", "row", "sec"),
        P(("sec", "gx", "row"), None),
        P(("sec", "gx", "row"), None, None),
        P(("sec", "gx", "row")),
        P(("sec", "gx", "row")),
        P("sec", "gx", "row"),
        P(("sec", "gx", "row")),
        P(None, ("sec", "gx", "row")),
    )
    out_specs = (P(None, "gx", "row", "sec"), P(None, "gx", "row", "sec"), P())
    return jax.shard_map(
        per_device, mesh=mesh, in_specs=in_specs, out_specs=out_specs, check_vma=False
    )
```

```python
import jax
import jax.numpy as jnp
from jax import lax
from jax.experimental import pallas as pl
from jax.experimental.pallas import tpu as pltpu
from jax.sharding import PartitionSpec as P

LES_STEP = 0.2
WAVE_STEP = 0.25
CAP = 10
ROWS = 17
F32 = jnp.float32
BF16 = jnp.bfloat16
ALL = ("sec", "gx", "row")
MIB = 1 << 20


def iota(shape, dim):
    return lax.broadcasted_iota(jnp.int32, shape, dim)


def as_column(line):
    return jnp.transpose(jnp.broadcast_to(line, (128, 128)))


def edge_line(block, lane, eye):
    return jnp.sum(jnp.where(eye, block[:, lane : lane + 1], 0.0), axis=0, keepdims=True)


def safe(density):
    return jnp.where(density == 0.0, 1.0, density)


def down(plane, halo):
    return jnp.where(iota(plane.shape, 0) == 0, halo, pltpu.roll(plane, 1, 0))


def up(plane, halo):
    last = plane.shape[0] - 1
    return jnp.where(iota(plane.shape, 0) == last, halo, pltpu.roll(plane, last, 0))


def derive_z(plane, halo, sec):
    lane = iota(plane.shape, 1)
    before = jnp.where(lane == 0, jnp.where(sec == 1, halo, 0.0), pltpu.roll(plane, 1, 1))
    after = jnp.where(lane == 127, jnp.where(sec == 0, halo, 0.0), pltpu.roll(plane, 127, 1))
    return 0.5 * (after - before)


def even(axis):
    return lax.rem(lax.axis_index(axis), 2) == 0


def pack_x_kernel(rho, rest, wave, far, x_even, x_odd, landed):
    index = even("gx")
    copies = []
    for order, (target, upper) in enumerate(((x_even, index), (x_odd, jnp.logical_not(index)))):
        at = pl.multiple_of(jnp.where(upper, 480, 0), 32)
        wave_at = pl.multiple_of(jnp.where(upper, 112, 0), 16)
        moves = [(rho.at[pl.ds(at, 32)], target.at[0:32])]
        for part in range(4):
            here = target.at[32 * part + 32 : 32 * part + 64]
            moves.append((rest.at[pl.ds(part * 512 + at, 32)], here))
            here = target.at[16 * part + 160 : 16 * part + 176]
            moves.append((wave.at[pl.ds(part * 128 + wave_at, 16)], here))
        for k, (here, there) in enumerate(moves):
            copies.append(pltpu.make_async_copy(here, there, landed.at[order, k]))
    for copy in copies:
        copy.start()
    for copy in copies:
        copy.wait()


def pack_kernel(rho, rest, wave, y_even, y_odd, z_face):
    high = lax.axis_index("sec") == 0
    index = even("row")
    eye = iota((128, 128), 0) == iota((128, 128), 1)

    def pick(ref, start, count, width, upper):
        return ref[pl.ds(start + jnp.where(upper, width - 1, 0), count, stride=width)]

    for target, upper in ((y_even, index), (y_odd, jnp.logical_not(index))):
        target[0:16] = pick(rho, 0, 16, 32, upper)
        for part in range(4):
            target[16 * part + 16 : 16 * part + 32] = pick(rest, part * 512, 16, 32, upper)
        target[80:88] = pick(wave, 0, 8, 16, upper)
        target[88:96] = pick(wave, 256, 8, 16, upper)
    blocks = [(rho, piece) for piece in range(4)] + [(rest, piece) for piece in range(16)]
    blocks += [(wave, 0), (wave, 3)]
    for lane, here in ((127, high), (0, jnp.logical_not(high))):
        @pl.when(here)
        def _():
            for line, (ref, piece) in enumerate(blocks):
                z_face[line : line + 1] = edge_line(
                    ref[piece * 128 : piece * 128 + 128], lane, eye
                )
    z_face[22:24] = jnp.zeros((2, 128), F32)


def sides(x_even, x_odd, y_even, y_odd):
    x_index, y_index = even("gx"), even("row")
    return (
        jnp.where(x_index, x_odd[...], x_even[...]),
        jnp.where(x_index, x_even[...], x_odd[...]),
        jnp.where(y_index, y_odd[...], y_even[...]),
        jnp.where(y_index, y_even[...], y_odd[...]),
    )


def slot_kernel(owner, counts, patch, weights, slots, valid, patches):
    below = iota((128, 128), 0) < iota((128, 128), 1)
    target = iota((128, 128), 0) * 16
    lane = iota((128, 128), 1)
    lines = [owner[piece : piece + 1].astype(F32) for piece in range(4)]
    columns = [as_column(line) for line in lines]
    for piece in range(4):
        rank = jnp.zeros((1, 128), F32)
        for other in range(piece + 1):
            same = columns[other] == lines[piece]
            if other == piece:
                same = same & below
            rank = rank + jnp.sum(same.astype(F32), axis=0, keepdims=True)
        code = (lines[piece] * 16.0 + rank).astype(jnp.int32)
        here = slice(piece * 128, piece * 128 + 128)
        for slot in range(CAP):
            hit = (target + slot) == code
            slots[slot * 128 : slot * 128 + 128, here] = hit.astype(F32).astype(BF16)
        limit = as_column(counts[piece : piece + 1].astype(F32))
        valid[here] = (lane.astype(F32) < limit).astype(F32)
        patches[here] = as_column(patch[piece : piece + 1].astype(F32)).astype(BF16)


def payload_kernel(
    rho, momentum, x_even, x_odd, y_even, y_odd, z_face, valid, weights,
    payload, speed, z_speed, y_speed,
):
    sec = lax.axis_index("sec")

    x_low, x_high, y_low, y_high = sides(x_even, x_odd, y_even, y_odd)
    for side, face in enumerate((y_low, y_high)):
        for k, part in enumerate((0, 2)):
            y_speed[2 * side + k] = face[16 * part + 16 : 16 * part + 32] / safe(face[0:16])
    inverse = 1.0 / rho[...]
    for part in range(3):
        speed[part, 32:544] = momentum[part * 512 : part * 512 + 512] * inverse
        for at, face in ((0, x_low), (544, x_high)):
            speed[part, at : at + 32] = (
                face[32 * part + 32 : 32 * part + 64] / safe(face[0:32])
            )
    for part in range(2):
        edge = z_face[4 * part + 4 : 4 * part + 8] / safe(z_face[0:4])
        for piece in range(4):
            z_speed[part, piece * 128 : piece * 128 + 128] = as_column(edge[piece : piece + 1])

    group = iota((16, 128), 0)
    half = iota((16, 128), 1) < 64
    keep = [(group // 4 == part).astype(F32).astype(BF16) for part in range(4)]
    column = iota((64, 48), 1) % 4

    for x in range(16):
        at = x * 32
        v = [speed[part, pl.ds(at + 32, 32)] for part in range(3)]
        v_before = [speed[part, pl.ds(at, 32)] for part in range(3)]
        v_after = [speed[part, pl.ds(at + 64, 32)] for part in range(3)]
        y_before = {part: y_speed[part // 2, pl.ds(x, 1)] for part in (0, 2)}
        y_after = {part: y_speed[2 + part // 2, pl.ds(x, 1)] for part in (0, 2)}
        along = {part: 0.5 * (v_after[part] - v_before[part]) for part in (1, 2)}
        across = {
            part: 0.5 * (up(v[part], y_after[part]) - down(v[part], y_before[part]))
            for part in (0, 2)
        }
        deep = {part: derive_z(v[part], z_speed[part, pl.ds(at, 32)], sec) for part in (0, 1)}
        swirl_x = across[2] - deep[1]
        swirl_y = deep[0] - along[2]
        swirl_z = along[1] - across[0]
        mask = valid[pl.ds(at, 32)]
        lamb = [
            ((swirl_y * v[2] - swirl_z * v[1]) * mask).astype(BF16),
            ((swirl_z * v[0] - swirl_x * v[2]) * mask).astype(BF16),
            ((swirl_x * v[1] - swirl_y * v[0]) * mask).astype(BF16),
        ]
        for part in range(2):
            rows = slice(part * 16, part * 16 + 16)
            left = jnp.concatenate(
                [
                    jnp.concatenate([lamb[c][rows] * keep[k] for k in range(4)], axis=1)
                    for c in range(3)
                ],
                axis=0,
            )
            first = (x * 32 + part * 16) * 64
            right = jnp.concatenate(
                [
                    weights[first + 256 * k : first + 256 * k + 256]
                    for k in range(4)
                ],
                axis=1,
            )
            product = lax.dot_general(
                right, left, (((1,), (1,)), ((), ())), preferred_element_type=F32
            )
            merged = product[0:64]
            for k in range(1, 4):
                merged = jnp.where(column == k, product[k * 64 : k * 64 + 64], merged)
            turned = jnp.transpose(jnp.concatenate([merged, merged], axis=0))
            folded = [turned[c * 16 : c * 16 + 16] for c in range(3)]
            pair = jnp.where(half, folded[0], folded[1])
            pair_top = pair.astype(BF16)
            pair_rest = (pair - pair_top.astype(F32)).astype(BF16)
            single_top = folded[2].astype(BF16).astype(F32)
            single = jnp.where(half, single_top, folded[2] - single_top).astype(BF16)
            here = slice(at + part * 16, at + part * 16 + 16)
            payload[here, 0:128] = pair_top
            payload[here, 128:256] = pair_rest
            payload[here, 256:384] = single


def place_kernel(slots, payload, patches, share, other, send, rows, sent):
    half = iota((32, 128), 1) < 64
    lane = iota((32, 128), 1)
    values = jnp.concatenate([payload[...], patches[...]], axis=1)
    both = jnp.broadcast_to(share[0:1] + other[0:1], (32, 128))
    copies = []
    for block in range(4):
        hits = [slots[slot * 128 + block * 32 : slot * 128 + block * 32 + 32] for slot in range(CAP)]
        placed = jnp.dot(jnp.concatenate(hits, axis=0), values, preferred_element_type=F32)
        first = block * 32 * ROWS
        numbers = jnp.zeros((32, 128), F32)
        for slot in range(CAP):
            mine = placed[slot * 32 : slot * 32 + 32]
            rows[pl.ds(first + slot, 32, stride=ROWS)] = mine[:, 0:128] + mine[:, 128:256]
            third = mine[:, 256:384]
            third = third + pltpu.roll(third, 64, 1)
            if slot % 2 == 0:
                kept = third
            else:
                rows[pl.ds(first + CAP + slot // 2, 32, stride=ROWS)] = jnp.where(
                    half, kept, third
                )
            numbers = jnp.where(lane == slot, mine[:, 384:512], numbers)
        rows[pl.ds(first + CAP * 3 // 2, 32, stride=ROWS)] = numbers
        rows[pl.ds(first + CAP * 3 // 2 + 1, 32, stride=ROWS)] = both
        here = pl.ds(first, 32 * ROWS)
        copy = pltpu.make_async_copy(rows.at[here], send.at[here], sent.at[block])
        copy.start()
        copies.append(copy)
    for copy in copies:
        copy.wait()


def wave_kernel(
    tile_class, wave, x_even, x_odd, y_even, y_odd, z_face, samples, far, base, share
):
    sec = lax.axis_index("sec")
    x_low, x_high, y_low, y_high = sides(x_even, x_odd, y_even, y_odd)
    level = tile_class[0, 0].astype(F32)
    mean_flow = 0.1 + 0.3 * level
    stiffness = 1.0 + 0.25 * level
    z_pressure = as_column(z_face[20:21])
    z_speed = as_column(z_face[21:22])
    for x in range(8):
        def row(part, at):
            start = part * 128 + at * 16
            if at < 0:
                return x_low[160 + 16 * part : 176 + 16 * part]
            if at > 7:
                return x_high[160 + 16 * part : 176 + 16 * part]
            return wave[start : start + 16]

        now = [row(part, x) for part in range(4)]
        along = [0.5 * (row(part, x + 1) - row(part, x - 1)) for part in range(4)]
        across = [
            0.5
            * (
                up(now[part], y_high[80 + 8 * k + x : 81 + 8 * k + x])
                - down(now[part], y_low[80 + 8 * k + x : 81 + 8 * k + x])
            )
            for k, part in enumerate((0, 2))
        ]
        here = slice(x * 16, x * 16 + 16)
        deep = [derive_z(now[0], z_pressure[here], sec), derive_z(now[3], z_speed[here], sec)]
        divergence = along[1] + across[1] + deep[1]
        base[here] = now[0] - WAVE_STEP * (mean_flow * along[0] + stiffness * divergence)
        for part, gradient in ((1, along[0]), (2, across[0]), (3, deep[0])):
            base[part * 128 + x * 16 : part * 128 + x * 16 + 16] = now[part] - WAVE_STEP * (
                mean_flow * along[part] + gradient
            )
    index = samples[...]
    line, cell = index // 128, index % 128
    picks = (iota((128, 128), 0) == line).astype(F32)
    columns = lax.dot_general(
        base[0:128], picks, (((0,), (0,)), ((), ())),
        precision=lax.Precision.HIGHEST, preferred_element_type=F32,
    )
    values = jnp.sum(
        jnp.where(iota((128, 128), 0) == cell, columns, 0.0), axis=0, keepdims=True
    )
    share[...] = lax.dot_general(
        jnp.broadcast_to(values, (8, 128)), far[...], (((1,), (1,)), ((), ())),
        precision=lax.Precision.HIGHEST, preferred_element_type=F32,
    )


def les_kernel(rho, rest, x_even, x_odd, y_even, y_odd, z_face, out):
    sec = lax.axis_index("sec")
    x_low, x_high, y_low, y_high = sides(x_even, x_odd, y_even, y_odd)
    lane = iota((32, 128), 1)
    z_rho = safe(z_face[0:4])
    z_v = z_face[12:16] / z_rho
    y_low_v = y_low[32:48] / safe(y_low[0:16])
    y_high_v = y_high[32:48] / safe(y_high[0:16])
    x_low_v = x_low[32:64] / safe(x_low[0:32])
    x_high_v = x_high[32:64] / safe(x_high[0:32])
    for part in range(5):
        def state(x):
            if part == 0:
                return rho[x * 32 : x * 32 + 32]
            return rest[part * 512 - 512 + x * 32 : part * 512 - 512 + x * 32 + 32]

        z_flux = z_face[4 * part : 4 * part + 4] * z_v
        y_low_flux = y_low[16 * part : 16 * part + 16] * y_low_v
        y_high_flux = y_high[16 * part : 16 * part + 16] * y_high_v
        for x in range(16):
            density = rho[x * 32 : x * 32 + 32]
            now = state(x)

            def stream(at):
                if at < 0:
                    return x_low[32 * part : 32 * part + 32] * x_low_v
                if at > 15:
                    return x_high[32 * part : 32 * part + 32] * x_high_v
                return state(at) * (rest[at * 32 : at * 32 + 32] / rho[at * 32 : at * 32 + 32])

            along = 0.5 * (stream(x + 1) - stream(x - 1))
            side = now * (rest[512 + x * 32 : 512 + x * 32 + 32] / density)
            across = 0.5 * (
                up(side, y_high_flux[x : x + 1]) - down(side, y_low_flux[x : x + 1])
            )
            depth = now * (rest[1024 + x * 32 : 1024 + x * 32 + 32] / density)
            if x % 4 == 0:
                z_column = as_column(z_flux[x // 4 : x // 4 + 1])
            deep = derive_z(depth, z_column[x % 4 * 32 : x % 4 * 32 + 32], sec)
            start = part * 512 + x * 32
            out[start : start + 32] = now - LES_STEP * (along + across + deep)


def finish_kernel(arrived, base, out, far):
    names = jnp.transpose(arrived[pl.ds(CAP * 3 // 2, 128, stride=ROWS)])
    place = iota((256, 128), 0)
    patch = (place % 128 * 2 + place // 128).astype(F32)
    half = iota((128, 128), 1) < 64
    total = jnp.zeros((256, 512), F32)
    for pair in range(CAP // 2):
        third = arrived[pl.ds(CAP + pair, 128, stride=ROWS)]
        left, right = [], []
        for slot in (2 * pair, 2 * pair + 1):
            left.append((patch == names[slot : slot + 1]).astype(F32).astype(BF16))
            both = arrived[pl.ds(slot, 128, stride=ROWS)]
            one = jnp.where(half == (slot % 2 == 0), third, 0.0)
            row = []
            for value in (both, one):
                top = value.astype(BF16)
                row += [top, (value - top.astype(F32)).astype(BF16)]
            right.append(jnp.concatenate(row, axis=1))
        total = total + jnp.dot(
            jnp.concatenate(left, axis=1),
            jnp.concatenate(right, axis=0),
            preferred_element_type=F32,
        )
    both = total[:, 0:128] + total[:, 128:256]
    third = total[:, 256:384] + total[:, 384:512]
    third = third + pltpu.roll(third, 64, 1)
    even, odd = both[0:128], both[128:256]
    source = [
        jnp.where(half, even, pltpu.roll(odd, 64, 1)),
        jnp.where(half, pltpu.roll(even, 64, 1), odd),
        jnp.where(half, third[0:128], third[128:256]),
    ]
    out[0:128] = base[0:128]
    for part in range(3):
        here = slice(part * 128 + 128, part * 128 + 256)
        out[here] = base[here] - WAVE_STEP * source[part]
    shares = arrived[pl.ds(CAP * 3 // 2 + 1, 128, stride=ROWS)]
    far[...] = jnp.sum(shares, axis=0, keepdims=True)


def call(kernel, outs, flops, moved, limit=16, **more):
    return pl.pallas_call(
        kernel,
        out_shape=[jax.ShapeDtypeStruct(shape, kind) for shape, kind in outs],
        compiler_params=pltpu.CompilerParams(vmem_limit_bytes=limit * MIB),
        cost_estimate=pl.CostEstimate(flops=flops, bytes_accessed=moved, transcendentals=0),
        **more,
    )


def exchange(face, axis, first):
    pairs = []
    for low in range(first, lax.axis_size(axis) - 1, 2):
        pairs += [(low, low + 1), (low + 1, low)]
    return lax.ppermute(face, axis, pairs)


def per_device(
    les_density,
    les_rest,
    acoustic,
    block_owner,
    block_weights,
    block_counts,
    block_patch,
    tile_class,
    sample_index,
    far_kernel,
):
    rho = les_density.reshape(512, 128)
    rest = les_rest.reshape(2048, 128)
    wave = acoustic.reshape(512, 128)
    weights = block_weights.reshape(512 * 64, 128)
    hbm = pl.BlockSpec(memory_space=pltpu.HBM)
    vmem = pl.BlockSpec(memory_space=pltpu.VMEM)
    smem = pl.BlockSpec(memory_space=pltpu.SMEM)
    pinned = lambda x: pltpu.with_memory_space_constraint(x, pltpu.HBM)
    with jax.named_scope("pack_x"):
        faces = call(
            pack_x_kernel,
            [((224, 128), F32)] * 2,
            1 << 10, 1 << 20,
            in_specs=[hbm] * 4,
            scratch_shapes=[pltpu.SemaphoreType.DMA((2, 9))],
        )(pinned(rho), pinned(rest), pinned(wave), pinned(far_kernel))
    x_even = exchange(faces[0], "gx", 0)
    x_odd = exchange(faces[1], "gx", 1)
    with jax.named_scope("pack"):
        faces = call(
            pack_kernel,
            [((96, 128), F32)] * 2 + [((24, 128), F32)],
            1 << 20, 2 << 20,
        )(rho, rest, wave)
    y_even = exchange(faces[0], "row", 0)
    y_odd = exchange(faces[1], "row", 1)
    z_face = exchange(faces[2], "sec", 0)
    halos = [x_even, x_odd, y_even, y_odd, z_face]
    with jax.named_scope("slots"):
        slots, valid, patches = call(
            slot_kernel,
            [((CAP * 128, 512), BF16), ((512, 128), F32), ((512, 128), BF16)],
            1 << 22, 2 << 20,
            in_specs=[vmem] * 3 + [hbm],
        )(
            block_owner.reshape(4, 128),
            block_counts.reshape(4, 128),
            block_patch.reshape(4, 128),
            pinned(weights),
        )
    with jax.named_scope("wave"):
        base, share = call(
            wave_kernel,
            [((512, 128), F32), ((8, 128), F32)],
            1 << 24, 2 << 20,
            in_specs=[smem] + [vmem] * 8,
        )(
            tile_class.reshape(1, 1), wave, *halos, sample_index.reshape(1, 128), far_kernel
        )
    other = exchange(share, "sec", 0)
    with jax.named_scope("payload"):
        (payload,) = call(
            payload_kernel,
            [((512, 384), BF16)],
            1 << 27, 16 << 20, 24,
            in_specs=[vmem] * 9,
            scratch_shapes=[
                pltpu.VMEM((3, 576, 128), F32),
                pltpu.VMEM((2, 512, 128), F32),
                pltpu.VMEM((4, 16, 128), F32),
            ],
        )(rho, rest, *halos, valid, weights)
    with jax.named_scope("place"):
        (send,) = call(
            place_kernel,
            [((128 * ROWS, 128), F32)],
            1 << 28, 3 << 20,
            out_specs=[hbm],
            scratch_shapes=[
                pltpu.VMEM((128 * ROWS, 128), F32),
                pltpu.SemaphoreType.DMA((4,)),
            ],
        )(slots, payload, patches, share, other)
    arrived = lax.all_to_all(
        send.reshape(128, 1, ROWS * 128), ("gx", "row"), split_axis=0, concat_axis=0, tiled=True
    )
    with jax.named_scope("les"):
        (les_next,) = call(les_kernel, [((2560, 128), F32)], 1 << 23, 4 << 20)(rho, rest, *halos)
    with jax.named_scope("finish"):
        wave_next, far_field = call(
            finish_kernel, [((512, 128), F32), ((1, 128), F32)], 1 << 28, 3 << 20,
        )(arrived.reshape(128 * ROWS, 128), base)
    return (
        les_next.reshape(5, 16, 32, 128),
        wave_next.reshape(4, 8, 16, 128),
        far_field.reshape(128),
    )


def solution(mesh):
    in_specs = (
        P("gx", "row", "sec"),
        P(None, "gx", "row", "sec"),
        P(None, "gx", "row", "sec"),
        P(("sec", "gx", "row"), None),
        P(("sec", "gx", "row"), None, None),
        P(("sec", "gx", "row")),
        P(("sec", "gx", "row")),
        P("sec", "gx", "row"),
        P(("sec", "gx", "row")),
        P(None, ("sec", "gx", "row")),
    )
    out_specs = (P(None, "gx", "row", "sec"), P(None, "gx", "row", "sec"), P())
    return jax.shard_map(
        per_device, mesh=mesh, in_specs=in_specs, out_specs=out_specs, check_vma=False
    )
```

```python
import jax
import jax.numpy as jnp
from jax import lax
from jax.experimental import pallas as pl
from jax.experimental.pallas import tpu as pltpu
from jax.sharding import PartitionSpec as P

LES_STEP = 0.2
WAVE_STEP = 0.25
CAP = 10
ROWS = 17
F32 = jnp.float32
BF16 = jnp.bfloat16
ALL = ("sec", "gx", "row")
MIB = 1 << 20


def iota(shape, dim):
    return lax.broadcasted_iota(jnp.int32, shape, dim)


def as_column(line):
    return jnp.transpose(jnp.broadcast_to(line, (128, 128)))


def edge_line(block, lane, eye):
    return jnp.sum(jnp.where(eye, block[:, lane : lane + 1], 0.0), axis=0, keepdims=True)


def safe(density):
    return jnp.where(density == 0.0, 1.0, density)


def down(plane, halo):
    return jnp.where(iota(plane.shape, 0) == 0, halo, pltpu.roll(plane, 1, 0))


def up(plane, halo):
    last = plane.shape[0] - 1
    return jnp.where(iota(plane.shape, 0) == last, halo, pltpu.roll(plane, last, 0))


def derive_z(plane, halo, sec):
    lane = iota(plane.shape, 1)
    before = jnp.where(lane == 0, jnp.where(sec == 1, halo, 0.0), pltpu.roll(plane, 1, 1))
    after = jnp.where(lane == 127, jnp.where(sec == 0, halo, 0.0), pltpu.roll(plane, 127, 1))
    return 0.5 * (after - before)


def even(axis):
    return lax.rem(lax.axis_index(axis), 2) == 0


def pack_y_kernel(rho, rest, wave, far, y_even, y_odd, low, high, wave_low, wave_high, landed):
    moves = [
        (rho.at[:, 0:8], low.at[0]), (rho.at[:, 24:32], high.at[0]),
        (rest.at[:, :, 0:8], low.at[1:5]), (rest.at[:, :, 24:32], high.at[1:5]),
    ]
    for k, part in enumerate((0, 2)):
        moves.append((wave.at[part, :, 0:8], wave_low.at[k]))
        moves.append((wave.at[part, :, 8:16], wave_high.at[k]))
    copies = [
        pltpu.make_async_copy(here, there, landed.at[k]) for k, (here, there) in enumerate(moves)
    ]
    for copy in copies:
        copy.start()
    for copy in copies:
        copy.wait()
    upper = even("row")
    lines = [(16 * part, 16, low[part, :, 0], high[part, :, 7]) for part in range(5)]
    lines += [(80 + 8 * part, 8, wave_low[part, :, 0], wave_high[part, :, 7]) for part in range(2)]
    for at, count, first, last in lines:
        y_even[at : at + count] = jnp.where(upper, last, first)
        y_odd[at : at + count] = jnp.where(upper, first, last)
    y_even[96:104] = jnp.zeros((8, 128), F32)
    y_odd[96:104] = jnp.zeros((8, 128), F32)


def pack_kernel(rho, rest, wave, weights, after, x_odd, x_even, z_face):
    index = even("gx")
    for target, upper in ((x_even, index), (x_odd, jnp.logical_not(index))):
        at = pl.multiple_of(jnp.where(upper, 480, 0), 32)
        wave_at = pl.multiple_of(jnp.where(upper, 112, 0), 16)
        inverse = 1.0 / rho[pl.ds(at, 32)]
        for k in range(2):
            target[32 * k : 32 * k + 32] = rest[pl.ds(512 * k + 512 + at, 32)] * inverse
            target[64 + 16 * k : 80 + 16 * k] = wave[pl.ds(128 * k + wave_at, 16)]
    high = lax.axis_index("sec") == 0
    eye = iota((128, 128), 0) == iota((128, 128), 1)
    blocks = [(rho, piece) for piece in range(4)] + [(rest, piece) for piece in range(16)]
    blocks += [(wave, 0), (wave, 3)]
    for lane, here in ((127, high), (0, jnp.logical_not(high))):
        @pl.when(here)
        def _():
            for line, (ref, piece) in enumerate(blocks):
                z_face[line : line + 1] = edge_line(
                    ref[piece * 128 : piece * 128 + 128], lane, eye
                )
    z_face[22:24] = jnp.zeros((2, 128), F32)


def late_kernel(rho, rest, wave, token, x_odd, x_even):
    index = even("gx")
    for target, upper in ((x_even, index), (x_odd, jnp.logical_not(index))):
        at = pl.multiple_of(jnp.where(upper, 480, 0), 32)
        wave_at = pl.multiple_of(jnp.where(upper, 112, 0), 16)
        target[0:32] = rho[pl.ds(at, 32)]
        for part in range(4):
            target[32 * part + 32 : 32 * part + 64] = rest[pl.ds(part * 512 + at, 32)]
        for k in range(2):
            target[160 + 16 * k : 176 + 16 * k] = wave[pl.ds(128 * k + 256 + wave_at, 16)]


def sides(x_even, x_odd, y_even, y_odd):
    x_index, y_index = even("gx"), even("row")
    return (
        jnp.where(x_index, x_odd[...], x_even[...]),
        jnp.where(x_index, x_even[...], x_odd[...]),
        jnp.where(y_index, y_odd[...], y_even[...]),
        jnp.where(y_index, y_even[...], y_odd[...]),
    )


def slot_kernel(owner, counts, patch, slots, valid, patches):
    below = iota((128, 128), 0) < iota((128, 128), 1)
    target = iota((128, 128), 0) * 16
    lane = iota((128, 128), 1)
    lines = [owner[piece : piece + 1].astype(F32) for piece in range(4)]
    columns = [as_column(line) for line in lines]
    for piece in range(4):
        rank = jnp.zeros((1, 128), F32)
        for other in range(piece + 1):
            same = columns[other] == lines[piece]
            if other == piece:
                same = same & below
            rank = rank + jnp.sum(same.astype(F32), axis=0, keepdims=True)
        code = (lines[piece] * 16.0 + rank).astype(jnp.int32)
        here = slice(piece * 128, piece * 128 + 128)
        for slot in range(CAP):
            hit = (target + slot) == code
            slots[slot * 128 : slot * 128 + 128, here] = hit.astype(F32).astype(BF16)
        limit = as_column(counts[piece : piece + 1].astype(F32))
        valid[here] = (lane.astype(F32) < limit).astype(F32)
        patches[here] = as_column(patch[piece : piece + 1].astype(F32)).astype(BF16)


def payload_kernel(
    rho, momentum, y_odd, y_even, x_odd, x_even, z_face, valid, weights,
    payload, speed, z_speed, y_speed,
):
    sec = lax.axis_index("sec")

    x_low, x_high, y_low, y_high = sides(x_even, x_odd, y_even, y_odd)
    for side, face in enumerate((y_low, y_high)):
        for k, part in enumerate((0, 2)):
            y_speed[2 * side + k] = face[16 * part + 16 : 16 * part + 32] / safe(face[0:16])
    inverse = 1.0 / rho[...]
    for part in range(3):
        speed[part, 32:544] = momentum[part * 512 : part * 512 + 512] * inverse
    for part in range(2):
        for at, face in ((0, x_low), (544, x_high)):
            speed[part + 1, at : at + 32] = face[32 * part : 32 * part + 32]
    for part in range(2):
        edge = z_face[4 * part + 4 : 4 * part + 8] / safe(z_face[0:4])
        for piece in range(4):
            z_speed[part, piece * 128 : piece * 128 + 128] = as_column(edge[piece : piece + 1])

    group = iota((16, 128), 0)
    half = iota((16, 128), 1) < 64
    keep = [(group // 4 == part).astype(F32).astype(BF16) for part in range(4)]
    column = iota((64, 48), 1) % 4

    for x in range(16):
        at = x * 32
        v = [speed[part, pl.ds(at + 32, 32)] for part in range(3)]
        v_before = [speed[part, pl.ds(at, 32)] for part in range(3)]
        v_after = [speed[part, pl.ds(at + 64, 32)] for part in range(3)]
        y_before = {part: y_speed[part // 2, pl.ds(x, 1)] for part in (0, 2)}
        y_after = {part: y_speed[2 + part // 2, pl.ds(x, 1)] for part in (0, 2)}
        along = {part: 0.5 * (v_after[part] - v_before[part]) for part in (1, 2)}
        across = {
            part: 0.5 * (up(v[part], y_after[part]) - down(v[part], y_before[part]))
            for part in (0, 2)
        }
        deep = {part: derive_z(v[part], z_speed[part, pl.ds(at, 32)], sec) for part in (0, 1)}
        swirl_x = across[2] - deep[1]
        swirl_y = deep[0] - along[2]
        swirl_z = along[1] - across[0]
        mask = valid[pl.ds(at, 32)]
        lamb = [
            ((swirl_y * v[2] - swirl_z * v[1]) * mask).astype(BF16),
            ((swirl_z * v[0] - swirl_x * v[2]) * mask).astype(BF16),
            ((swirl_x * v[1] - swirl_y * v[0]) * mask).astype(BF16),
        ]
        for part in range(2):
            rows = slice(part * 16, part * 16 + 16)
            left = jnp.concatenate(
                [
                    jnp.concatenate([lamb[c][rows] * keep[k] for k in range(4)], axis=1)
                    for c in range(3)
                ],
                axis=0,
            )
            first = (x * 32 + part * 16) * 64
            right = jnp.concatenate(
                [
                    weights[first + 256 * k : first + 256 * k + 256]
                    for k in range(4)
                ],
                axis=1,
            )
            product = lax.dot_general(
                right, left, (((1,), (1,)), ((), ())), preferred_element_type=F32
            )
            merged = product[0:64]
            for k in range(1, 4):
                merged = jnp.where(column == k, product[k * 64 : k * 64 + 64], merged)
            turned = jnp.transpose(jnp.concatenate([merged, merged], axis=0))
            folded = [turned[c * 16 : c * 16 + 16] for c in range(3)]
            pair = jnp.where(half, folded[0], folded[1])
            pair_top = pair.astype(BF16)
            pair_rest = (pair - pair_top.astype(F32)).astype(BF16)
            single_top = folded[2].astype(BF16).astype(F32)
            single = jnp.where(half, single_top, folded[2] - single_top).astype(BF16)
            here = slice(at + part * 16, at + part * 16 + 16)
            payload[here, 0:128] = pair_top
            payload[here, 128:256] = pair_rest
            payload[here, 256:384] = single


def place_kernel(slots, payload, patches, share, other, send, rows, sent):
    half = iota((32, 128), 1) < 64
    lane = iota((32, 128), 1)
    values = jnp.concatenate([payload[...], patches[...]], axis=1)
    both = jnp.broadcast_to(share[0:1] + other[0:1], (32, 128))
    copies = []
    for block in range(4):
        hits = [slots[slot * 128 + block * 32 : slot * 128 + block * 32 + 32] for slot in range(CAP)]
        placed = jnp.dot(jnp.concatenate(hits, axis=0), values, preferred_element_type=F32)
        first = block * 32 * ROWS
        numbers = jnp.zeros((32, 128), F32)
        for slot in range(CAP):
            mine = placed[slot * 32 : slot * 32 + 32]
            rows[pl.ds(first + slot, 32, stride=ROWS)] = mine[:, 0:128] + mine[:, 128:256]
            third = mine[:, 256:384]
            third = third + pltpu.roll(third, 64, 1)
            if slot % 2 == 0:
                kept = third
            else:
                rows[pl.ds(first + CAP + slot // 2, 32, stride=ROWS)] = jnp.where(
                    half, kept, third
                )
            numbers = jnp.where(lane == slot, mine[:, 384:512], numbers)
        rows[pl.ds(first + CAP * 3 // 2, 32, stride=ROWS)] = numbers
        rows[pl.ds(first + CAP * 3 // 2 + 1, 32, stride=ROWS)] = both
        here = pl.ds(first, 32 * ROWS)
        copy = pltpu.make_async_copy(rows.at[here], send.at[here], sent.at[block])
        copy.start()
        copies.append(copy)
    for copy in copies:
        copy.wait()


def factors(level):
    number = level[...].astype(F32)
    return 0.1 + 0.3 * number, 1.0 + 0.25 * number


def pressure_kernel(
    level, wave, y_odd, y_even, x_odd, x_even, z_face, samples, far, base, share
):
    sec = lax.axis_index("sec")
    x_low, x_high, y_low, y_high = sides(x_even, x_odd, y_even, y_odd)
    mean_flow, stiffness = factors(level)
    z_speed = as_column(z_face[21:22])
    for x in range(8):
        def row(part, at):
            if at < 0:
                return x_low[64 + 16 * part : 80 + 16 * part]
            if at > 7:
                return x_high[64 + 16 * part : 80 + 16 * part]
            return wave[part * 128 + at * 16 : part * 128 + at * 16 + 16]

        here = slice(x * 16, x * 16 + 16)
        along = [0.5 * (row(part, x + 1) - row(part, x - 1)) for part in range(2)]
        side = wave[256 + x * 16 : 272 + x * 16]
        across = 0.5 * (up(side, y_high[88 + x : 89 + x]) - down(side, y_low[88 + x : 89 + x]))
        deep = derive_z(wave[384 + x * 16 : 400 + x * 16], z_speed[here], sec)
        divergence = along[1] + across + deep
        base[here] = wave[here] - WAVE_STEP * (mean_flow * along[0] + stiffness * divergence)
    index = samples[...]
    line, cell = index // 128, index % 128
    picks = (iota((128, 128), 0) == line).astype(F32)
    columns = lax.dot_general(
        base[...], picks, (((0,), (0,)), ((), ())),
        precision=lax.Precision.HIGHEST, preferred_element_type=F32,
    )
    values = jnp.sum(
        jnp.where(iota((128, 128), 0) == cell, columns, 0.0), axis=0, keepdims=True
    )
    share[...] = lax.dot_general(
        jnp.broadcast_to(values, (8, 128)), far[...], (((1,), (1,)), ((), ())),
        precision=lax.Precision.HIGHEST, preferred_element_type=F32,
    )


def les_kernel(
    level, rho, rest, wave, y_odd, y_even, x_odd, x_even, z_face, late_odd, late_even, out, base
):
    sec = lax.axis_index("sec")
    x_low, x_high, y_low, y_high = sides(x_even, x_odd, y_even, y_odd)
    below, above, _, _ = sides(late_even, late_odd, y_even, y_odd)
    mean_flow, _ = factors(level)
    z_pressure = as_column(z_face[20:21])
    for x in range(8):
        def row(part, at):
            if 0 <= at <= 7:
                return wave[part * 128 + at * 16 : part * 128 + at * 16 + 16]
            early, rest_of = (x_low, below) if at < 0 else (x_high, above)
            if part < 2:
                return early[64 + 16 * part : 80 + 16 * part]
            return rest_of[128 + 16 * part : 144 + 16 * part]

        now = row(0, x)
        across = 0.5 * (up(now, y_high[80 + x : 81 + x]) - down(now, y_low[80 + x : 81 + x]))
        deep = derive_z(now, z_pressure[x * 16 : x * 16 + 16], sec)
        along = [0.5 * (row(part, x + 1) - row(part, x - 1)) for part in range(4)]
        for part, gradient in ((1, along[0]), (2, across), (3, deep)):
            start = part * 128 - 128 + x * 16
            base[start : start + 16] = row(part, x) - WAVE_STEP * (
                mean_flow * along[part] + gradient
            )
    x_low, x_high = below, above
    z_rho = safe(z_face[0:4])
    z_v = z_face[12:16] / z_rho
    y_low_v = y_low[32:48] / safe(y_low[0:16])
    y_high_v = y_high[32:48] / safe(y_high[0:16])
    x_low_v = x_low[32:64] / safe(x_low[0:32])
    x_high_v = x_high[32:64] / safe(x_high[0:32])
    for part in range(5):
        def state(x):
            if part == 0:
                return rho[x * 32 : x * 32 + 32]
            return rest[part * 512 - 512 + x * 32 : part * 512 - 512 + x * 32 + 32]

        z_flux = z_face[4 * part : 4 * part + 4] * z_v
        y_low_flux = y_low[16 * part : 16 * part + 16] * y_low_v
        y_high_flux = y_high[16 * part : 16 * part + 16] * y_high_v
        for x in range(16):
            density = rho[x * 32 : x * 32 + 32]
            now = state(x)

            def stream(at):
                if at < 0:
                    return x_low[32 * part : 32 * part + 32] * x_low_v
                if at > 15:
                    return x_high[32 * part : 32 * part + 32] * x_high_v
                return state(at) * (rest[at * 32 : at * 32 + 32] / rho[at * 32 : at * 32 + 32])

            along = 0.5 * (stream(x + 1) - stream(x - 1))
            side = now * (rest[512 + x * 32 : 512 + x * 32 + 32] / density)
            across = 0.5 * (
                up(side, y_high_flux[x : x + 1]) - down(side, y_low_flux[x : x + 1])
            )
            depth = now * (rest[1024 + x * 32 : 1024 + x * 32 + 32] / density)
            if x % 4 == 0:
                z_column = as_column(z_flux[x // 4 : x // 4 + 1])
            deep = derive_z(depth, z_column[x % 4 * 32 : x % 4 * 32 + 32], sec)
            start = part * 512 + x * 32
            out[start : start + 32] = now - LES_STEP * (along + across + deep)


def finish_kernel(arrived, pressure, base, out, far):
    names = jnp.transpose(arrived[pl.ds(CAP * 3 // 2, 128, stride=ROWS)])
    place = iota((256, 128), 0)
    patch = (place % 128 * 2 + place // 128).astype(F32)
    half = iota((128, 128), 1) < 64
    total = jnp.zeros((256, 512), F32)
    for pair in range(CAP // 2):
        third = arrived[pl.ds(CAP + pair, 128, stride=ROWS)]
        left, right = [], []
        for slot in (2 * pair, 2 * pair + 1):
            left.append((patch == names[slot : slot + 1]).astype(F32).astype(BF16))
            both = arrived[pl.ds(slot, 128, stride=ROWS)]
            one = jnp.where(half == (slot % 2 == 0), third, 0.0)
            row = []
            for value in (both, one):
                top = value.astype(BF16)
                row += [top, (value - top.astype(F32)).astype(BF16)]
            right.append(jnp.concatenate(row, axis=1))
        total = total + jnp.dot(
            jnp.concatenate(left, axis=1),
            jnp.concatenate(right, axis=0),
            preferred_element_type=F32,
        )
    both = total[:, 0:128] + total[:, 128:256]
    third = total[:, 256:384] + total[:, 384:512]
    third = third + pltpu.roll(third, 64, 1)
    even, odd = both[0:128], both[128:256]
    source = [
        jnp.where(half, even, pltpu.roll(odd, 64, 1)),
        jnp.where(half, pltpu.roll(even, 64, 1), odd),
        jnp.where(half, third[0:128], third[128:256]),
    ]
    out[0:128] = pressure[...]
    for part in range(3):
        here = slice(part * 128, part * 128 + 128)
        out[part * 128 + 128 : part * 128 + 256] = base[here] - WAVE_STEP * source[part]
    shares = arrived[pl.ds(CAP * 3 // 2 + 1, 128, stride=ROWS)]
    far[...] = jnp.sum(shares, axis=0, keepdims=True)


def call(kernel, outs, flops, moved, limit=16, **more):
    return pl.pallas_call(
        kernel,
        out_shape=[jax.ShapeDtypeStruct(shape, kind) for shape, kind in outs],
        compiler_params=pltpu.CompilerParams(vmem_limit_bytes=limit * MIB),
        cost_estimate=pl.CostEstimate(flops=flops, bytes_accessed=moved, transcendentals=0),
        **more,
    )


def exchange(face, axis, first):
    pairs = []
    for low in range(first, lax.axis_size(axis) - 1, 2):
        pairs += [(low, low + 1), (low + 1, low)]
    return lax.ppermute(face, axis, pairs)


def per_device(
    les_density,
    les_rest,
    acoustic,
    block_owner,
    block_weights,
    block_counts,
    block_patch,
    tile_class,
    sample_index,
    far_kernel,
):
    rho = les_density.reshape(512, 128)
    rest = les_rest.reshape(2048, 128)
    wave = acoustic.reshape(512, 128)
    weights = block_weights.reshape(512 * 64, 128)
    hbm = pl.BlockSpec(memory_space=pltpu.HBM)
    vmem = pl.BlockSpec(memory_space=pltpu.VMEM)
    pinned = lambda x: pltpu.with_memory_space_constraint(x, pltpu.HBM)
    with jax.named_scope("pack_y"):
        y_even, y_odd = call(
            pack_y_kernel,
            [((104, 128), F32)] * 2,
            1 << 18, 1 << 20,
            in_specs=[hbm] * 4,
            scratch_shapes=[pltpu.VMEM((5, 16, 8, 128), F32)] * 2
            + [pltpu.VMEM((2, 8, 8, 128), F32)] * 2
            + [pltpu.SemaphoreType.DMA((8,))],
        )(pinned(les_density), pinned(les_rest), pinned(acoustic), pinned(far_kernel))
    with jax.named_scope("pack"):
        x_odd, x_even, z_face = call(
            pack_kernel,
            [((96, 128), F32)] * 2 + [((24, 128), F32)],
            1 << 20, 2 << 20,
            in_specs=[vmem] * 3 + [hbm, vmem],
        )(rho, rest, wave, pinned(weights), y_even)
    halos = [
        exchange(y_odd, "row", 1),
        exchange(y_even, "row", 0),
        exchange(x_odd, "gx", 1),
        exchange(x_even, "gx", 0),
        exchange(z_face, "sec", 0),
    ]
    with jax.named_scope("slots"):
        slots, valid, patches = call(
            slot_kernel,
            [((CAP * 128, 512), BF16), ((512, 128), F32), ((512, 128), BF16)],
            1 << 22, 2 << 20,
        )(
            block_owner.reshape(4, 128),
            block_counts.reshape(4, 128),
            block_patch.reshape(4, 128),
        )
    level = tile_class.reshape(1, 1)
    with jax.named_scope("pressure"):
        pressure, share = call(
            pressure_kernel, [((128, 128), F32), ((8, 128), F32)], 1 << 24, 2 << 20,
        )(level, wave, *halos, sample_index.reshape(1, 128), far_kernel)
    other = exchange(share, "sec", 0)
    with jax.named_scope("payload"):
        (payload,) = call(
            payload_kernel,
            [((512, 384), BF16)],
            1 << 27, 16 << 20, 24,
            in_specs=[vmem] * 9,
            scratch_shapes=[
                pltpu.VMEM((3, 576, 128), F32),
                pltpu.VMEM((2, 512, 128), F32),
                pltpu.VMEM((4, 16, 128), F32),
            ],
        )(rho, rest, *halos, valid, weights)
    with jax.named_scope("place"):
        (send,) = call(
            place_kernel,
            [((128 * ROWS, 128), F32)],
            1 << 28, 3 << 20,
            out_specs=[hbm],
            scratch_shapes=[
                pltpu.VMEM((128 * ROWS, 128), F32),
                pltpu.SemaphoreType.DMA((4,)),
            ],
        )(slots, payload, patches, share, other)
    arrived = lax.all_to_all(
        send.reshape(128, 1, ROWS * 128), ("gx", "row"), split_axis=0, concat_axis=0, tiled=True
    )
    with jax.named_scope("late"):
        late_odd, late_even = call(
            late_kernel, [((192, 128), F32)] * 2, 1 << 10, 1 << 19, in_specs=[vmem] * 3 + [hbm],
        )(rho, rest, wave, pinned(send))
    late_odd = exchange(late_odd, "gx", 1)
    late_even = exchange(late_even, "gx", 0)
    with jax.named_scope("les"):
        les_next, base = call(
            les_kernel, [((2560, 128), F32), ((384, 128), F32)], 1 << 23, 4 << 20
        )(level, rho, rest, wave, *halos, late_odd, late_even)
    with jax.named_scope("finish"):
        wave_next, far_field = call(
            finish_kernel, [((512, 128), F32), ((1, 128), F32)], 1 << 28, 3 << 20,
        )(arrived.reshape(128 * ROWS, 128), pressure, base)
    return (
        les_next.reshape(5, 16, 32, 128),
        wave_next.reshape(4, 8, 16, 128),
        far_field.reshape(128),
    )


def solution(mesh):
    in_specs = (
        P("gx", "row", "sec"),
        P(None, "gx", "row", "sec"),
        P(None, "gx", "row", "sec"),
        P(("sec", "gx", "row"), None),
        P(("sec", "gx", "row"), None, None),
        P(("sec", "gx", "row")),
        P(("sec", "gx", "row")),
        P("sec", "gx", "row"),
        P(("sec", "gx", "row")),
        P(None, ("sec", "gx", "row")),
    )
    out_specs = (P(None, "gx", "row", "sec"), P(None, "gx", "row", "sec"), P())
    return jax.shard_map(
        per_device, mesh=mesh, in_specs=in_specs, out_specs=out_specs, check_vma=False
    )
```

```python
import jax
import jax.numpy as jnp
from jax import lax
from jax.experimental import pallas as pl
from jax.experimental.pallas import tpu as pltpu
from jax.sharding import PartitionSpec as P

LES_STEP = 0.2
WAVE_STEP = 0.25
CAP = 10
ROWS = 17
F32 = jnp.float32
BF16 = jnp.bfloat16
ALL = ("sec", "gx", "row")
MIB = 1 << 20


def iota(shape, dim):
    return lax.broadcasted_iota(jnp.int32, shape, dim)


def as_column(line):
    return jnp.transpose(jnp.broadcast_to(line, (128, 128)))


def edge_line(block, lane, eye):
    return jnp.sum(jnp.where(eye, block[:, lane : lane + 1], 0.0), axis=0, keepdims=True)


def safe(density):
    return jnp.where(density == 0.0, 1.0, density)


def down(plane, halo):
    return jnp.where(iota(plane.shape, 0) == 0, halo, pltpu.roll(plane, 1, 0))


def up(plane, halo):
    last = plane.shape[0] - 1
    return jnp.where(iota(plane.shape, 0) == last, halo, pltpu.roll(plane, last, 0))


def derive_z(plane, halo, sec):
    lane = iota(plane.shape, 1)
    before = jnp.where(lane == 0, jnp.where(sec == 1, halo, 0.0), pltpu.roll(plane, 1, 1))
    after = jnp.where(lane == 127, jnp.where(sec == 0, halo, 0.0), pltpu.roll(plane, 127, 1))
    return 0.5 * (after - before)


def even(axis):
    return lax.rem(lax.axis_index(axis), 2) == 0


def pack_y_kernel(rho, rest, wave, far, y_even, y_odd, low, high, wave_low, wave_high, landed):
    moves = [
        (rho.at[:, 0:8], low.at[0]), (rho.at[:, 24:32], high.at[0]),
        (rest.at[:, :, 0:8], low.at[1:5]), (rest.at[:, :, 24:32], high.at[1:5]),
    ]
    for k, part in enumerate((0, 2)):
        moves.append((wave.at[part, :, 0:8], wave_low.at[k]))
        moves.append((wave.at[part, :, 8:16], wave_high.at[k]))
    copies = [
        pltpu.make_async_copy(here, there, landed.at[k]) for k, (here, there) in enumerate(moves)
    ]
    for copy in copies:
        copy.start()
    for copy in copies:
        copy.wait()
    upper = even("row")
    lines = [(16 * part, 16, low[part, :, 0], high[part, :, 7]) for part in range(5)]
    lines += [(80 + 8 * part, 8, wave_low[part, :, 0], wave_high[part, :, 7]) for part in range(2)]
    for at, count, first, last in lines:
        y_even[at : at + count] = jnp.where(upper, last, first)
        y_odd[at : at + count] = jnp.where(upper, first, last)
    y_even[96:104] = jnp.zeros((8, 128), F32)
    y_odd[96:104] = jnp.zeros((8, 128), F32)


def pack_kernel(rho, rest, wave, weights, after, x_odd, x_even, z_face):
    index = even("gx")
    for target, upper in ((x_even, index), (x_odd, jnp.logical_not(index))):
        at = pl.multiple_of(jnp.where(upper, 480, 0), 32)
        wave_at = pl.multiple_of(jnp.where(upper, 112, 0), 16)
        inverse = 1.0 / rho[pl.ds(at, 32)]
        for k in range(2):
            target[32 * k : 32 * k + 32] = rest[pl.ds(512 * k + 512 + at, 32)] * inverse
            target[64 + 16 * k : 80 + 16 * k] = wave[pl.ds(128 * k + wave_at, 16)]
    high = lax.axis_index("sec") == 0
    eye = iota((128, 128), 0) == iota((128, 128), 1)
    blocks = [(rho, piece) for piece in range(4)] + [(rest, piece) for piece in range(16)]
    blocks += [(wave, 0), (wave, 3)]
    for lane, here in ((127, high), (0, jnp.logical_not(high))):
        @pl.when(here)
        def _():
            for line, (ref, piece) in enumerate(blocks):
                z_face[line : line + 1] = edge_line(
                    ref[piece * 128 : piece * 128 + 128], lane, eye
                )
    z_face[22:100] = jnp.zeros((78, 128), F32)


def late_kernel(rho, rest, wave, token, x_odd, x_even):
    index = even("gx")
    for target, upper in ((x_even, index), (x_odd, jnp.logical_not(index))):
        at = pl.multiple_of(jnp.where(upper, 480, 0), 32)
        wave_at = pl.multiple_of(jnp.where(upper, 112, 0), 16)
        target[0:32] = rho[pl.ds(at, 32)]
        for part in range(4):
            target[32 * part + 32 : 32 * part + 64] = rest[pl.ds(part * 512 + at, 32)]
        for k in range(2):
            target[160 + 16 * k : 176 + 16 * k] = wave[pl.ds(128 * k + 256 + wave_at, 16)]


def sides(x_even, x_odd, y_even, y_odd):
    x_index, y_index = even("gx"), even("row")
    return (
        jnp.where(x_index, x_odd[...], x_even[...]),
        jnp.where(x_index, x_even[...], x_odd[...]),
        jnp.where(y_index, y_odd[...], y_even[...]),
        jnp.where(y_index, y_even[...], y_odd[...]),
    )


def slot_kernel(owner, counts, patch, slots, valid, patches):
    below = iota((128, 128), 0) < iota((128, 128), 1)
    target = iota((128, 128), 0) * 16
    lane = iota((128, 128), 1)
    lines = [owner[piece : piece + 1].astype(F32) for piece in range(4)]
    columns = [as_column(line) for line in lines]
    for piece in range(4):
        rank = jnp.zeros((1, 128), F32)
        for other in range(piece + 1):
            same = columns[other] == lines[piece]
            if other == piece:
                same = same & below
            rank = rank + jnp.sum(same.astype(F32), axis=0, keepdims=True)
        code = (lines[piece] * 16.0 + rank).astype(jnp.int32)
        here = slice(piece * 128, piece * 128 + 128)
        for slot in range(CAP):
            hit = (target + slot) == code
            slots[slot * 128 : slot * 128 + 128, here] = hit.astype(F32).astype(BF16)
        limit = as_column(counts[piece : piece + 1].astype(F32))
        valid[here] = (lane.astype(F32) < limit).astype(F32)
        patches[here] = as_column(patch[piece : piece + 1].astype(F32)).astype(BF16)


def payload_kernel(
    rho, momentum, y_odd, y_even, x_odd, x_even, z_face, valid, weights,
    payload, speed, z_speed, y_speed,
):
    sec = lax.axis_index("sec")

    x_low, x_high, y_low, y_high = sides(x_even, x_odd, y_even, y_odd)
    for side, face in enumerate((y_low, y_high)):
        for k, part in enumerate((0, 2)):
            y_speed[2 * side + k] = face[16 * part + 16 : 16 * part + 32] / safe(face[0:16])
    inverse = 1.0 / rho[...]
    for part in range(3):
        speed[part, 32:544] = momentum[part * 512 : part * 512 + 512] * inverse
    for part in range(2):
        for at, face in ((0, x_low), (544, x_high)):
            speed[part + 1, at : at + 32] = face[32 * part : 32 * part + 32]
    for part in range(2):
        edge = z_face[4 * part + 4 : 4 * part + 8] / safe(z_face[0:4])
        for piece in range(4):
            z_speed[part, piece * 128 : piece * 128 + 128] = as_column(edge[piece : piece + 1])

    group = iota((16, 128), 0)
    half = iota((16, 128), 1) < 64
    keep = [(group // 4 == part).astype(F32).astype(BF16) for part in range(4)]
    column = iota((64, 48), 1) % 4
    wide = iota((16, 256), 1) // 64 == iota((16, 256), 0) % 4

    for x in range(16):
        at = x * 32
        v = [speed[part, pl.ds(at + 32, 32)] for part in range(3)]
        v_before = [speed[part, pl.ds(at, 32)] for part in range(3)]
        v_after = [speed[part, pl.ds(at + 64, 32)] for part in range(3)]
        y_before = {part: y_speed[part // 2, pl.ds(x, 1)] for part in (0, 2)}
        y_after = {part: y_speed[2 + part // 2, pl.ds(x, 1)] for part in (0, 2)}
        along = {part: 0.5 * (v_after[part] - v_before[part]) for part in (1, 2)}
        across = {
            part: 0.5 * (up(v[part], y_after[part]) - down(v[part], y_before[part]))
            for part in (0, 2)
        }
        deep = {part: derive_z(v[part], z_speed[part, pl.ds(at, 32)], sec) for part in (0, 1)}
        swirl_x = across[2] - deep[1]
        swirl_y = deep[0] - along[2]
        swirl_z = along[1] - across[0]
        mask = valid[pl.ds(at, 32)]
        lamb = [
            ((swirl_y * v[2] - swirl_z * v[1]) * mask).astype(BF16),
            ((swirl_z * v[0] - swirl_x * v[2]) * mask).astype(BF16),
            ((swirl_x * v[1] - swirl_y * v[0]) * mask).astype(BF16),
        ]
        for part in range(2):
            rows = slice(part * 16, part * 16 + 16)
            left = jnp.concatenate(
                [
                    jnp.concatenate([lamb[c][rows] * keep[k] for k in range(4)], axis=1)
                    for c in range(3)
                ],
                axis=0,
            )
            first = (x * 32 + part * 16) * 64
            right = jnp.concatenate(
                [
                    weights[first + 256 * k : first + 256 * k + 256]
                    for k in range(4)
                ],
                axis=1,
            )
            if part == 1 or x % 2 == 1:
                product = lax.dot_general(
                    left, right, (((1,), (1,)), ((), ())), preferred_element_type=F32
                )
                folded = []
                for c in range(3):
                    picked = jnp.where(wide, product[c * 16 : c * 16 + 16], 0.0)
                    both = picked[:, 0:128] + picked[:, 128:256]
                    folded.append(both + pltpu.roll(both, 64, 1))
            else:
                product = lax.dot_general(
                    right, left, (((1,), (1,)), ((), ())), preferred_element_type=F32
                )
                merged = product[0:64]
                for k in range(1, 4):
                    merged = jnp.where(column == k, product[k * 64 : k * 64 + 64], merged)
                turned = jnp.transpose(jnp.concatenate([merged, merged], axis=0))
                folded = [turned[c * 16 : c * 16 + 16] for c in range(3)]
            pair = jnp.where(half, folded[0], folded[1])
            pair_top = pair.astype(BF16)
            pair_rest = (pair - pair_top.astype(F32)).astype(BF16)
            single_top = folded[2].astype(BF16).astype(F32)
            single = jnp.where(half, single_top, folded[2] - single_top).astype(BF16)
            here = slice(at + part * 16, at + part * 16 + 16)
            payload[here, 0:128] = pair_top
            payload[here, 128:256] = pair_rest
            payload[here, 256:384] = single


def place_kernel(slots, payload, patches, share, other, send, rows, sent):
    half = iota((32, 128), 1) < 64
    lane = iota((32, 128), 1)
    values = jnp.concatenate([payload[...], patches[...]], axis=1)
    both = jnp.broadcast_to(share[0:1] + other[0:1], (32, 128))
    copies = []
    for block in range(4):
        hits = [slots[slot * 128 + block * 32 : slot * 128 + block * 32 + 32] for slot in range(CAP)]
        placed = jnp.dot(jnp.concatenate(hits, axis=0), values, preferred_element_type=F32)
        first = block * 32 * ROWS
        numbers = jnp.zeros((32, 128), F32)
        for slot in range(CAP):
            mine = placed[slot * 32 : slot * 32 + 32]
            rows[pl.ds(first + slot, 32, stride=ROWS)] = mine[:, 0:128] + mine[:, 128:256]
            third = mine[:, 256:384]
            third = third + pltpu.roll(third, 64, 1)
            if slot % 2 == 0:
                kept = third
            else:
                rows[pl.ds(first + CAP + slot // 2, 32, stride=ROWS)] = jnp.where(
                    half, kept, third
                )
            numbers = jnp.where(lane == slot, mine[:, 384:512], numbers)
        rows[pl.ds(first + CAP * 3 // 2, 32, stride=ROWS)] = numbers
        rows[pl.ds(first + CAP * 3 // 2 + 1, 32, stride=ROWS)] = both
        here = pl.ds(first, 32 * ROWS)
        copy = pltpu.make_async_copy(rows.at[here], send.at[here], sent.at[block])
        copy.start()
        copies.append(copy)
    for copy in copies:
        copy.wait()


def factors(level):
    number = level[...].astype(F32)
    return 0.1 + 0.3 * number, 1.0 + 0.25 * number


def pressure_kernel(
    level, wave, y_odd, y_even, x_odd, x_even, z_face, samples, far, base, share
):
    sec = lax.axis_index("sec")
    x_low, x_high, y_low, y_high = sides(x_even, x_odd, y_even, y_odd)
    mean_flow, stiffness = factors(level)
    z_speed = as_column(z_face[21:22])
    for x in range(8):
        def row(part, at):
            if at < 0:
                return x_low[64 + 16 * part : 80 + 16 * part]
            if at > 7:
                return x_high[64 + 16 * part : 80 + 16 * part]
            return wave[part * 128 + at * 16 : part * 128 + at * 16 + 16]

        here = slice(x * 16, x * 16 + 16)
        along = [0.5 * (row(part, x + 1) - row(part, x - 1)) for part in range(2)]
        side = wave[256 + x * 16 : 272 + x * 16]
        across = 0.5 * (up(side, y_high[88 + x : 89 + x]) - down(side, y_low[88 + x : 89 + x]))
        deep = derive_z(wave[384 + x * 16 : 400 + x * 16], z_speed[here], sec)
        divergence = along[1] + across + deep
        base[here] = wave[here] - WAVE_STEP * (mean_flow * along[0] + stiffness * divergence)
    index = samples[...]
    line, cell = index // 128, index % 128
    picks = (iota((128, 128), 0) == line).astype(F32)
    columns = lax.dot_general(
        base[...], picks, (((0,), (0,)), ((), ())),
        precision=lax.Precision.HIGHEST, preferred_element_type=F32,
    )
    values = jnp.sum(
        jnp.where(iota((128, 128), 0) == cell, columns, 0.0), axis=0, keepdims=True
    )
    share[...] = lax.dot_general(
        jnp.broadcast_to(values, (8, 128)), far[...], (((1,), (1,)), ((), ())),
        precision=lax.Precision.HIGHEST, preferred_element_type=F32,
    )


def les_kernel(
    level, rho, rest, wave, y_odd, y_even, x_odd, x_even, z_face, late_odd, late_even, out, base
):
    sec = lax.axis_index("sec")
    x_low, x_high, y_low, y_high = sides(x_even, x_odd, y_even, y_odd)
    below, above, _, _ = sides(late_even, late_odd, y_even, y_odd)
    mean_flow, _ = factors(level)
    z_pressure = as_column(z_face[20:21])
    for x in range(8):
        def row(part, at):
            if 0 <= at <= 7:
                return wave[part * 128 + at * 16 : part * 128 + at * 16 + 16]
            early, rest_of = (x_low, below) if at < 0 else (x_high, above)
            if part < 2:
                return early[64 + 16 * part : 80 + 16 * part]
            return rest_of[128 + 16 * part : 144 + 16 * part]

        now = row(0, x)
        across = 0.5 * (up(now, y_high[80 + x : 81 + x]) - down(now, y_low[80 + x : 81 + x]))
        deep = derive_z(now, z_pressure[x * 16 : x * 16 + 16], sec)
        along = [0.5 * (row(part, x + 1) - row(part, x - 1)) for part in range(4)]
        for part, gradient in ((1, along[0]), (2, across), (3, deep)):
            start = part * 128 - 128 + x * 16
            base[start : start + 16] = row(part, x) - WAVE_STEP * (
                mean_flow * along[part] + gradient
            )
    x_low, x_high = below, above
    z_rho = safe(z_face[0:4])
    z_v = z_face[12:16] / z_rho
    y_low_v = y_low[32:48] / safe(y_low[0:16])
    y_high_v = y_high[32:48] / safe(y_high[0:16])
    x_low_v = x_low[32:64] / safe(x_low[0:32])
    x_high_v = x_high[32:64] / safe(x_high[0:32])
    for part in range(5):
        def state(x):
            if part == 0:
                return rho[x * 32 : x * 32 + 32]
            return rest[part * 512 - 512 + x * 32 : part * 512 - 512 + x * 32 + 32]

        z_flux = z_face[4 * part : 4 * part + 4] * z_v
        y_low_flux = y_low[16 * part : 16 * part + 16] * y_low_v
        y_high_flux = y_high[16 * part : 16 * part + 16] * y_high_v
        for x in range(16):
            density = rho[x * 32 : x * 32 + 32]
            now = state(x)

            def stream(at):
                if at < 0:
                    return x_low[32 * part : 32 * part + 32] * x_low_v
                if at > 15:
                    return x_high[32 * part : 32 * part + 32] * x_high_v
                return state(at) * (rest[at * 32 : at * 32 + 32] / rho[at * 32 : at * 32 + 32])

            along = 0.5 * (stream(x + 1) - stream(x - 1))
            side = now * (rest[512 + x * 32 : 512 + x * 32 + 32] / density)
            across = 0.5 * (
                up(side, y_high_flux[x : x + 1]) - down(side, y_low_flux[x : x + 1])
            )
            depth = now * (rest[1024 + x * 32 : 1024 + x * 32 + 32] / density)
            if x % 4 == 0:
                z_column = as_column(z_flux[x // 4 : x // 4 + 1])
            deep = derive_z(depth, z_column[x % 4 * 32 : x % 4 * 32 + 32], sec)
            start = part * 512 + x * 32
            out[start : start + 32] = now - LES_STEP * (along + across + deep)


def finish_kernel(arrived, pressure, base, out, far):
    names = jnp.transpose(arrived[pl.ds(CAP * 3 // 2, 128, stride=ROWS)])
    place = iota((256, 128), 0)
    patch = (place % 128 * 2 + place // 128).astype(F32)
    half = iota((128, 128), 1) < 64
    total = jnp.zeros((256, 512), F32)
    for pair in range(CAP // 2):
        third = arrived[pl.ds(CAP + pair, 128, stride=ROWS)]
        left, right = [], []
        for slot in (2 * pair, 2 * pair + 1):
            left.append((patch == names[slot : slot + 1]).astype(F32).astype(BF16))
            both = arrived[pl.ds(slot, 128, stride=ROWS)]
            one = jnp.where(half == (slot % 2 == 0), third, 0.0)
            row = []
            for value in (both, one):
                top = value.astype(BF16)
                row += [top, (value - top.astype(F32)).astype(BF16)]
            right.append(jnp.concatenate(row, axis=1))
        total = total + jnp.dot(
            jnp.concatenate(left, axis=1),
            jnp.concatenate(right, axis=0),
            preferred_element_type=F32,
        )
    both = total[:, 0:128] + total[:, 128:256]
    third = total[:, 256:384] + total[:, 384:512]
    third = third + pltpu.roll(third, 64, 1)
    even, odd = both[0:128], both[128:256]
    source = [
        jnp.where(half, even, pltpu.roll(odd, 64, 1)),
        jnp.where(half, pltpu.roll(even, 64, 1), odd),
        jnp.where(half, third[0:128], third[128:256]),
    ]
    out[0:128] = pressure[...]
    for part in range(3):
        here = slice(part * 128, part * 128 + 128)
        out[part * 128 + 128 : part * 128 + 256] = base[here] - WAVE_STEP * source[part]
    shares = arrived[pl.ds(CAP * 3 // 2 + 1, 128, stride=ROWS)]
    far[...] = jnp.sum(shares, axis=0, keepdims=True)


def call(kernel, outs, flops, moved, limit=16, **more):
    return pl.pallas_call(
        kernel,
        out_shape=[jax.ShapeDtypeStruct(shape, kind) for shape, kind in outs],
        compiler_params=pltpu.CompilerParams(vmem_limit_bytes=limit * MIB),
        cost_estimate=pl.CostEstimate(flops=flops, bytes_accessed=moved, transcendentals=0),
        **more,
    )


def exchange(face, axis, first):
    pairs = []
    for low in range(first, lax.axis_size(axis) - 1, 2):
        pairs += [(low, low + 1), (low + 1, low)]
    return lax.ppermute(face, axis, pairs)


def per_device(
    les_density,
    les_rest,
    acoustic,
    block_owner,
    block_weights,
    block_counts,
    block_patch,
    tile_class,
    sample_index,
    far_kernel,
):
    rho = les_density.reshape(512, 128)
    rest = les_rest.reshape(2048, 128)
    wave = acoustic.reshape(512, 128)
    weights = block_weights.reshape(512 * 64, 128)
    hbm = pl.BlockSpec(memory_space=pltpu.HBM)
    vmem = pl.BlockSpec(memory_space=pltpu.VMEM)
    pinned = lambda x: pltpu.with_memory_space_constraint(x, pltpu.HBM)
    with jax.named_scope("pack_y"):
        y_even, y_odd = call(
            pack_y_kernel,
            [((104, 128), F32)] * 2,
            1 << 18, 1 << 20,
            in_specs=[hbm] * 4,
            scratch_shapes=[pltpu.VMEM((5, 16, 8, 128), F32)] * 2
            + [pltpu.VMEM((2, 8, 8, 128), F32)] * 2
            + [pltpu.SemaphoreType.DMA((8,))],
        )(pinned(les_density), pinned(les_rest), pinned(acoustic), pinned(far_kernel))
    with jax.named_scope("pack"):
        x_odd, x_even, z_face = call(
            pack_kernel,
            [((96, 128), F32)] * 2 + [((100, 128), F32)],
            1 << 20, 2 << 20,
            in_specs=[vmem] * 3 + [hbm, vmem],
        )(rho, rest, wave, pinned(weights), y_even)
    halos = [
        exchange(y_odd, "row", 1),
        exchange(y_even, "row", 0),
        exchange(x_odd, "gx", 1),
        exchange(x_even, "gx", 0),
        exchange(z_face, "sec", 0),
    ]
    with jax.named_scope("slots"):
        slots, valid, patches = call(
            slot_kernel,
            [((CAP * 128, 512), BF16), ((512, 128), F32), ((512, 128), BF16)],
            1 << 22, 2 << 20,
        )(
            block_owner.reshape(4, 128),
            block_counts.reshape(4, 128),
            block_patch.reshape(4, 128),
        )
    level = tile_class.reshape(1, 1)
    with jax.named_scope("pressure"):
        pressure, share = call(
            pressure_kernel, [((128, 128), F32), ((8, 128), F32)], 1 << 24, 2 << 20,
        )(level, wave, *halos, sample_index.reshape(1, 128), far_kernel)
    other = exchange(share, "sec", 0)
    with jax.named_scope("payload"):
        (payload,) = call(
            payload_kernel,
            [((512, 384), BF16)],
            1 << 27, 16 << 20, 24,
            in_specs=[vmem] * 9,
            scratch_shapes=[
                pltpu.VMEM((3, 576, 128), F32),
                pltpu.VMEM((2, 512, 128), F32),
                pltpu.VMEM((4, 16, 128), F32),
            ],
        )(rho, rest, *halos, valid, weights)
    with jax.named_scope("place"):
        (send,) = call(
            place_kernel,
            [((128 * ROWS, 128), F32)],
            1 << 28, 3 << 20,
            out_specs=[hbm],
            scratch_shapes=[
                pltpu.VMEM((128 * ROWS, 128), F32),
                pltpu.SemaphoreType.DMA((4,)),
            ],
        )(slots, payload, patches, share, other)
    arrived = lax.all_to_all(
        send.reshape(128, 1, ROWS * 128), ("gx", "row"), split_axis=0, concat_axis=0, tiled=True
    )
    with jax.named_scope("late"):
        late_odd, late_even = call(
            late_kernel, [((192, 128), F32)] * 2, 1 << 10, 1 << 19, in_specs=[vmem] * 3 + [hbm],
        )(rho, rest, wave, pinned(send))
    late_odd = exchange(late_odd, "gx", 1)
    late_even = exchange(late_even, "gx", 0)
    with jax.named_scope("les"):
        les_next, base = call(
            les_kernel, [((2560, 128), F32), ((384, 128), F32)], 1 << 23, 4 << 20
        )(level, rho, rest, wave, *halos, late_odd, late_even)
    with jax.named_scope("finish"):
        wave_next, far_field = call(
            finish_kernel, [((512, 128), F32), ((1, 128), F32)], 1 << 28, 3 << 20,
        )(arrived.reshape(128 * ROWS, 128), pressure, base)
    return (
        les_next.reshape(5, 16, 32, 128),
        wave_next.reshape(4, 8, 16, 128),
        far_field.reshape(128),
    )


def solution(mesh):
    in_specs = (
        P("gx", "row", "sec"),
        P(None, "gx", "row", "sec"),
        P(None, "gx", "row", "sec"),
        P(("sec", "gx", "row"), None),
        P(("sec", "gx", "row"), None, None),
        P(("sec", "gx", "row")),
        P(("sec", "gx", "row")),
        P("sec", "gx", "row"),
        P(("sec", "gx", "row")),
        P(None, ("sec", "gx", "row")),
    )
    out_specs = (P(None, "gx", "row", "sec"), P(None, "gx", "row", "sec"), P())
    return jax.shard_map(
        per_device, mesh=mesh, in_specs=in_specs, out_specs=out_specs, check_vma=False
    )
```
